512 devices in a mesh: grp: 16 (over z), ctx: 32 (over x, y, core).
Axes of the slice: x: 4, y: 4, z: 16, core: 2. Of those that a mesh axis runs over, the one named last changes fastest.
Arguments:
- query_vectors: bfloat16 [131072, 1536], P(('grp', 'ctx')), may hold values from -8 to 8
- key_vectors: bfloat16 [131072, 1536], P(('grp', 'ctx')), may hold values from -8 to 8
- value_vectors: bfloat16 [131072, 1536], P(('grp', 'ctx')), may hold values from -6 to 6
- chosen_groups: int32 [16, 8, 2], replicated, may hold values from -2 to 14, as said below
- chosen_count: int32 [16, 8], replicated, may hold values from 0 to 2, as said below
Outputs:
- attended: bfloat16 [131072, 1536], P(('grp', 'ctx'))
The draws below stay inside these ranges and needn't reach their ends.
Inputs may be any that keep to these rules, and one draw needn't show every extreme that they name: For j < chosen_count[g, w] the entries chosen_groups[g, w, j] are distinct groups from g - 2 to g - 1, none below 0; later entries carry no meaning. chosen_count[g, w] is at most min(g, 2) and equals 2 for some window of the last group.
All inputs are finite; a program needn't handle non-finite values.
Results may differ from the reference program's by a relative error of at most 0.0041.
Values may be sent and summed in bfloat16 or wider, within the bound.
No kernel may reach another device: no remote copies, remote signals or barrier semaphores. Data moves between devices by JAX's collectives and lax.ppermute only.
A program may use at most 128 MiB of HBM per device.

```python
import jax
import jax.numpy as jnp
from jax import lax

HEADS = 12
HD = 128
POS = 256
SPAN = 4
FG = 32
PD = 8
NWIN = 8
LOOK = 2
TOKENS = 131072
N_GRP = 16


def draw_query_vectors(key, part):
    key = jax.random.fold_in(key, 1)
    return jnp.clip(jax.random.normal(key, (TOKENS, HEADS * HD), jnp.float32), -6.0, 6.0).astype(jnp.bfloat16)


def draw_key_vectors(key, part):
    key = jax.random.fold_in(key, 2)
    return jnp.clip(jax.random.normal(key, (TOKENS, HEADS * HD), jnp.float32), -6.0, 6.0).astype(jnp.bfloat16)


def draw_chosen_count(key, part):
    key = jax.random.fold_in(key, 3)
    drawn = jax.random.randint(key, (N_GRP, NWIN), 0, LOOK + 1)
    groups = jnp.arange(N_GRP, dtype=jnp.int32)[:, None]
    counts = jnp.minimum(drawn, groups)
    column = jax.random.randint(jax.random.fold_in(key, 5), (), 0, NWIN)
    forced = (groups == N_GRP - 1) & (jnp.arange(NWIN, dtype=jnp.int32)[None, :] == column)
    return jnp.where(forced, LOOK, counts).astype(jnp.int32)


def draw_chosen_groups(key, part):
    key = jax.random.fold_in(key, 4)
    jitter = jax.random.randint(key, (N_GRP, NWIN, LOOK), 0, 4096)
    offsets = jnp.arange(LOOK, dtype=jnp.int32)[None, None, :]
    groups = jnp.arange(N_GRP, dtype=jnp.int32)[:, None, None]
    beyond = (offsets >= groups).astype(jnp.int32)
    scores = beyond * (8192 * LOOK) + jitter * LOOK + offsets
    ranking = jnp.argsort(scores, axis=-1, stable=True).astype(jnp.int32)
    return (groups - 1 - ranking).astype(jnp.int32)


def block_scale(stream_key, shape, split, smallest, high):
    def one(position, parts):
        draws = jax.random.uniform(jax.random.fold_in(jax.random.fold_in(stream_key, 6), position), (parts,), jnp.float32, smallest / len(split), high / len(split))
        return jnp.repeat(jnp.exp(draws), shape[position] // parts).reshape((-1,) + (1,) * (len(shape) - position - 1))

    factor_of = one(*split[0])
    for cut in split[1:]:
        factor_of = factor_of * one(*cut)
    return factor_of


def centred(stream_key, extent, scale, limit, pieces=(), held_as=jnp.bfloat16):
    array = scale * jax.random.normal(stream_key, extent, jnp.float32)
    if pieces:
        array = array * block_scale(stream_key, extent, pieces, -0.22, 0.18)
    return jnp.clip(array, -limit, limit).astype(held_as)


def setup_inputs(seed: int = 0) -> dict:
    streams_of = jax.random.split(jax.random.key(seed), 6)
    return {
        "query_vectors": draw_query_vectors(jax.random.fold_in(streams_of[5], 71), 0),
        "key_vectors": draw_key_vectors(jax.random.fold_in(streams_of[5], 71), 0),
        "value_vectors": centred(streams_of[2], (TOKENS, HEADS * HD), 1.0, 6.0, ((0, 512),)),
        "chosen_groups": draw_chosen_groups(jax.random.fold_in(streams_of[5], 71), 0),
        "chosen_count": draw_chosen_count(jax.random.fold_in(streams_of[5], 71), 0),
    }


NEG_FILL = -1e30


def split_blocks(matrix):
    shaped = matrix.reshape(N_GRP, FG, NWIN, SPAN, PD, HEADS, HD)
    return jnp.transpose(shaped, (0, 2, 3, 5, 1, 4, 6))


def tile_partial(query_tile, key_tile, value_tile, causal):
    query_wide = query_tile.astype(jnp.float32).reshape(HEADS, SPAN * FG * PD, HD)
    key_wide = key_tile.astype(jnp.float32).reshape(HEADS, FG * PD, HD)
    value_wide = value_tile.astype(jnp.float32).reshape(HEADS, FG * PD, HD)
    scores = jnp.einsum('hqd,hkd->hqk', query_wide, key_wide, precision=lax.Precision.HIGHEST) * (HD ** -0.5)
    if causal:
        frame_query = (lax.broadcasted_iota(jnp.int32, (SPAN * FG * PD, FG * PD), 0) // PD) % FG
        frame_key = lax.broadcasted_iota(jnp.int32, (SPAN * FG * PD, FG * PD), 1) // PD
        scores = jnp.where((frame_query >= frame_key)[None, :, :], scores, NEG_FILL)
    highest = jnp.max(scores, axis=-1)
    weights = jnp.exp(scores - highest[:, :, None])
    summed = jnp.sum(weights, axis=-1)
    rounded = lax.optimization_barrier(weights.astype(jnp.bfloat16)).astype(jnp.float32)
    blended = jnp.einsum('hqk,hkd->hqd', rounded, value_wide, precision=lax.Precision.HIGHEST)
    return (highest, summed, blended)


def combine(left_part, right_part):
    ceiling = jnp.maximum(left_part[0], right_part[0])
    left_scale = jnp.exp(left_part[0] - ceiling)
    right_scale = jnp.exp(right_part[0] - ceiling)
    summed = left_part[1] * left_scale + right_part[1] * right_scale
    blended = left_part[2] * left_scale[..., None] + right_part[2] * right_scale[..., None]
    return (ceiling, summed, blended)


def reference(query_vectors, key_vectors, value_vectors, chosen_groups, chosen_count):
    query_blocks = split_blocks(query_vectors)
    key_blocks = split_blocks(key_vectors)
    value_blocks = split_blocks(value_vectors)

    def one_block(flat_index):
        group_id = flat_index // NWIN
        window_id = flat_index % NWIN
        query_tile = jnp.transpose(query_blocks[group_id, window_id], (1, 0, 2, 3, 4))

        def window_partial(source, causal):
            running = tile_partial(query_tile, key_blocks[source, window_id, 0], value_blocks[source, window_id, 0], causal)
            for block_id in range(1, SPAN):
                running = combine(running, tile_partial(query_tile, key_blocks[source, window_id, block_id], value_blocks[source, window_id, block_id], causal))
            return running

        running = window_partial(group_id, True)
        picked = chosen_groups[group_id, window_id]
        limit_count = chosen_count[group_id, window_id]
        slot_ids = jnp.arange(LOOK, dtype=jnp.int32)
        for distance in range(1, LOOK + 1):
            source = group_id - distance
            taken = jnp.any((picked == source) & (slot_ids < limit_count)) & (source >= 0)
            clipped = jnp.maximum(source, 0).astype(jnp.int32)

            def absorb(current, clipped=clipped):
                return combine(current, window_partial(clipped, False))

            running = lax.cond(taken, absorb, lambda current: current, running)
        blended = running[2] / running[1][:, :, None]
        return blended.astype(jnp.bfloat16).reshape(HEADS, SPAN, FG, PD, HD)

    outputs = lax.map(one_block, jnp.arange(N_GRP * NWIN, dtype=jnp.int32))
    outputs = outputs.reshape(N_GRP, NWIN, HEADS, SPAN, FG, PD, HD)
    outputs = jnp.transpose(outputs, (0, 4, 1, 3, 5, 2, 6))
    return outputs.reshape(N_GRP * FG * POS, HEADS * HD)
```

```python
import functools
import math

import jax
import jax.numpy as jnp
from jax import lax
from jax.experimental import pallas as pl
from jax.experimental.pallas import tpu as pltpu
from jax.sharding import PartitionSpec as P

HEADS = 12
HD = 128
POS = 256
SPAN = 4
NWIN = 8
LOOK = 2
QB = 256
PARTS = HEADS // SPAN
POSITIONS = POS // NWIN
STAT_ROWS = 32
LOG2E = math.log2(math.e)
FACTOR = HD**-0.5 * LOG2E
NEG_FILL = -1e30
SMEM = pl.BlockSpec(memory_space=pltpu.SMEM)
VMEM = pl.BlockSpec(memory_space=pltpu.VMEM)
ANY = pl.BlockSpec(memory_space=pl.ANY)
PARAMS = pltpu.CompilerParams(vmem_limit_bytes=32 * 2**20)


def is_taken(groups_ref, count_ref, group, distance):
    groups = groups_ref.shape[0]
    window = lax.axis_index("ctx") // SPAN
    held = jnp.minimum(group, groups - 1)
    source = group - distance
    count = count_ref[held, window]
    taken = jnp.bool_(False)
    for slot in range(LOOK):
        taken = taken | ((groups_ref[held, window, slot] == source) & (slot < count))
    return taken & (source >= 0) & (group < groups)


def softmax_part(query, keys, values, diagonal):
    scores = lax.dot_general(
        query, keys, (((1,), (1,)), ((), ())), preferred_element_type=jnp.float32
    )
    if diagonal:
        rows, count = scores.shape
        tail = scores[:, count - rows :]
        frame_query = lax.broadcasted_iota(jnp.int32, (rows, rows), 0) // POSITIONS
        frame_key = lax.broadcasted_iota(jnp.int32, (rows, rows), 1) // POSITIONS
        tail = jnp.where(frame_query >= frame_key, tail, NEG_FILL)
        scores = jnp.concatenate([scores[:, : count - rows], tail], axis=1) if count > rows else tail
    highest = jnp.max(scores, axis=-1, keepdims=True)
    weights = jnp.exp2((scores - highest) * FACTOR)
    summed = jnp.sum(weights, axis=-1, keepdims=True)
    blended = jnp.dot(weights.astype(jnp.bfloat16), values, preferred_element_type=jnp.float32)
    return highest, summed, blended


def join(old, new):
    ceiling = jnp.maximum(old[0], new[0])
    old_scale = jnp.exp2((old[0] - ceiling) * FACTOR)
    new_scale = jnp.exp2((new[0] - ceiling) * FACTOR)
    return (
        ceiling,
        old[1] * old_scale + new[1] * new_scale,
        old[2] * old_scale + new[2] * new_scale,
    )


def rows_of(ref, slab, start, size):
    first, count = start // POSITIONS, size // POSITIONS
    return ref[pl.ds(first, count), slab].reshape(size, HD)


def eye_mask():
    return lax.broadcasted_iota(jnp.int32, (HD, HD), 0) == lax.broadcasted_iota(
        jnp.int32, (HD, HD), 1
    )


def log_rows(part):
    log_sum = part[0] * FACTOR + jnp.log(part[1]) * LOG2E
    return [
        jnp.sum(jnp.where(eye_mask(), log_sum[at : at + HD], 0.0), axis=0, keepdims=True)
        for at in range(0, log_sum.shape[0], HD)
    ]


def ahead_kernel(groups_ref, count_ref, q_ref, kv_ref, out_ref):
    rows = q_ref.shape[0] * POSITIONS
    taken = is_taken(groups_ref, count_ref, lax.axis_index("grp") + 1, 2)

    @pl.when(taken)
    def _():
        for head in range(q_ref.shape[1]):
            keys = rows_of(kv_ref, 2 * head, 0, rows)
            values = rows_of(kv_ref, 2 * head + 1, 0, rows)
            logs = []
            for start in range(0, rows, QB):
                query = rows_of(q_ref, head, start, QB)
                part = softmax_part(query, keys, values, False)
                out_ref[head, pl.ds(start, QB), :] = (part[2] / part[1]).astype(jnp.bfloat16)
                logs += log_rows(part)
            left = jnp.concatenate(logs, axis=0)
            pieces = []
            for _ in range(3):
                pieces.append(left.astype(jnp.bfloat16).astype(jnp.float32))
                left = left - pieces[-1]
            pieces.append(jnp.zeros((STAT_ROWS - 3 * len(logs), HD), jnp.float32))
            packed = jnp.concatenate(pieces, axis=0).astype(jnp.bfloat16)
            out_ref[head, pl.ds(rows, STAT_ROWS), :] = packed

    @pl.when(jnp.logical_not(taken))
    def _():
        out_ref[...] = jnp.zeros_like(out_ref)


def near_kernel(
    groups_ref, count_ref, first_ref, second_ref, first_up_ref, second_up_ref, out_ref, log_ref
):
    rows = first_ref.shape[0] * POSITIONS
    taken = is_taken(groups_ref, count_ref, lax.axis_index("grp"), 1)

    def pair_of(first, second, head, size):
        ref, slab = (first, 2 * head) if head < 2 else (second, 0)
        return rows_of(ref, slab, 0, size), rows_of(ref, slab + 1, 0, size)

    def put(head, start, part):
        out_ref[head, pl.ds(start, QB), :] = part[2] / part[1]
        for at, row in enumerate(log_rows(part)):
            log_ref[head, pl.ds(start // HD + at, 1), :] = row

    def own(head, start):
        query = rows_of(second_ref, 2 + head, start, QB)
        return softmax_part(query, *pair_of(first_ref, second_ref, head, start + QB), True)

    @pl.when(taken)
    def _():
        for head in range(PARTS):
            for start in range(0, rows, QB):
                query = rows_of(second_ref, 2 + head, start, QB)
                earlier = softmax_part(
                    query, *pair_of(first_up_ref, second_up_ref, head, rows), False
                )
                put(head, start, join(own(head, start), earlier))

    @pl.when(jnp.logical_not(taken))
    def _():
        for head in range(PARTS):
            for start in range(0, rows, QB):
                put(head, start, own(head, start))


def merge_kernel(
    groups_ref, count_ref, near_ref, log_ref, first_far_ref, second_far_ref, out_ref
):
    rows = near_ref.shape[1]
    blocks = rows // HD
    taken = is_taken(groups_ref, count_ref, lax.axis_index("grp"), 2)

    def put(head, start, value):
        out_ref[pl.ds(start // POSITIONS, HD // POSITIONS), head] = value.astype(
            jnp.bfloat16
        ).reshape(HD // POSITIONS, POSITIONS, HD)

    @pl.when(taken)
    def _():
        for head in range(PARTS):
            far_ref = first_far_ref.at[head] if head < 2 else second_far_ref.at[0]
            pieces = far_ref[pl.ds(rows, STAT_ROWS), :].astype(jnp.float32)
            far_log = pieces[:blocks] + pieces[blocks : 2 * blocks] + pieces[2 * blocks : 3 * blocks]
            shares = 1.0 / (1.0 + jnp.exp2(log_ref[head] - far_log))
            for block in range(blocks):
                share = jnp.sum(
                    jnp.where(eye_mask(), shares[block : block + 1], 0.0), axis=1, keepdims=True
                )
                part = pl.ds(block * HD, HD)
                near = near_ref[head, part, :]
                far = far_ref[part, :].astype(jnp.float32)
                put(head, block * HD, near + (far - near) * share)

    @pl.when(jnp.logical_not(taken))
    def _():
        for head in range(PARTS):
            for start in range(0, rows, HD):
                put(head, start, near_ref[head, pl.ds(start, HD), :])


def cost(passes, rows, heads, moved):
    return pl.CostEstimate(
        flops=int(4 * passes * rows * rows * heads * HD),
        bytes_accessed=moved,
        transcendentals=int(passes * rows * rows * heads),
    )


def attend_ahead(groups, count, query, pair):
    rows, heads = query.shape[0] * POSITIONS, query.shape[1]
    return pl.pallas_call(
        ahead_kernel,
        in_specs=[SMEM] * 2 + [VMEM] * 2,
        out_specs=VMEM,
        out_shape=jax.ShapeDtypeStruct((heads, rows + STAT_ROWS, HD), jnp.bfloat16),
        compiler_params=PARAMS,
        cost_estimate=cost(1, rows, heads, rows * heads * HD * 8),
        name="ahead",
    )(groups, count, query, pair)


def attend_near(groups, count, first, second, first_up, second_up):
    rows = first.shape[0] * POSITIONS
    return pl.pallas_call(
        near_kernel,
        in_specs=[SMEM] * 2 + [VMEM] * 4,
        out_specs=[VMEM] * 2,
        out_shape=[
            jax.ShapeDtypeStruct((PARTS, rows, HD), jnp.float32),
            jax.ShapeDtypeStruct((PARTS, rows // HD, HD), jnp.float32),
        ],
        compiler_params=PARAMS,
        cost_estimate=cost(1.6, rows, PARTS, rows * PARTS * HD * 14),
        name="near",
    )(groups, count, first, second, first_up, second_up)


def merge(groups, count, near, logs, first_far, second_far):
    frames = near.shape[1] // POSITIONS
    return pl.pallas_call(
        merge_kernel,
        in_specs=[SMEM] * 2 + [VMEM] * 4,
        out_specs=VMEM,
        out_shape=jax.ShapeDtypeStruct((frames, PARTS, POSITIONS, HD), jnp.bfloat16),
        compiler_params=PARAMS,
        cost_estimate=cost(0, frames * POSITIONS, PARTS, frames * POSITIONS * PARTS * HD * 8),
        name="merge",
    )(groups, count, near, logs, first_far, second_far)


def cut_kernel(slabs, *refs):
    sources, out_ref = refs[:-1], refs[-1]
    for window in range(NWIN):
        rows = pl.ds(window * POSITIONS, POSITIONS)
        for part in range(SPAN):
            for slab, (source, head) in enumerate(slabs):
                lanes = pl.ds((part * PARTS + head) * HD, HD)
                out_ref[window * SPAN + part, slab] = sources[source][rows, lanes]


def cut(sources, slabs):
    return pl.pallas_call(
        functools.partial(cut_kernel, slabs),
        in_specs=[VMEM] * len(sources),
        out_specs=VMEM,
        out_shape=jax.ShapeDtypeStruct((NWIN * SPAN, len(slabs), POSITIONS, HD), jnp.bfloat16),
        compiler_params=PARAMS,
        name="cut",
    )(*sources)


def paste_kernel(in_ref, out_ref, held_ref, sems):
    copies = []
    for window in range(NWIN):
        rows = pl.ds(window * POSITIONS, POSITIONS)
        for part in range(SPAN):
            for head in range(PARTS):
                lanes = pl.ds((part * PARTS + head) * HD, HD)
                held_ref[rows, lanes] = in_ref[window * SPAN + part, head]
        copies.append(
            pltpu.make_async_copy(held_ref.at[rows], out_ref.at[rows], sems.at[window])
        )
        copies[-1].start()
    for copy in copies:
        copy.wait()


def paste(pieces):
    return pl.pallas_call(
        paste_kernel,
        in_specs=[VMEM],
        out_specs=ANY,
        out_shape=jax.ShapeDtypeStruct((POS, HEADS * HD), jnp.bfloat16),
        scratch_shapes=[
            pltpu.VMEM((POS, HEADS * HD), jnp.bfloat16),
            pltpu.SemaphoreType.DMA((NWIN,)),
        ],
        compiler_params=PARAMS,
        name="paste",
    )(pieces)


def body(query_vectors, key_vectors, value_vectors, chosen_groups, chosen_count):
    group_devices = lax.axis_size("grp")

    def to_peers(block):
        return lax.all_to_all(block, "ctx", split_axis=0, concat_axis=0, tiled=True)

    def up(block):
        return lax.ppermute(block, "grp", [(at, at + 1) for at in range(group_devices - 1)])

    def down(block):
        return lax.ppermute(block, "grp", [(at + 1, at) for at in range(group_devices - 1)])

    first = to_peers(cut((key_vectors, value_vectors), ((0, 0), (1, 0), (0, 1), (1, 1))))
    second = cut(
        (key_vectors, value_vectors, query_vectors), ((0, 2), (1, 2), (2, 0), (2, 1), (2, 2))
    )
    first, second = lax.optimization_barrier((first, second))
    first_up = up(first)
    second = to_peers(second)
    first_query = down(second[:, 2:4])
    second_up = up(second[:, 0:2])
    second_query = down(second[:, 4:5])
    first_far = up(attend_ahead(chosen_groups, chosen_count, first_query, first_up))
    second_far = up(attend_ahead(chosen_groups, chosen_count, second_query, second_up))
    near, logs = attend_near(chosen_groups, chosen_count, first, second, first_up, second_up)
    return paste(to_peers(merge(chosen_groups, chosen_count, near, logs, first_far, second_far)))


def solution(mesh):
    in_specs = (P(("grp", "ctx"), None), P(("grp", "ctx"), None), P(("grp", "ctx"), None), P(), P())
    out_specs = P(("grp", "ctx"), None)
    return jax.shard_map(body, mesh=mesh, in_specs=in_specs, out_specs=out_specs, check_vma=False)
```

```python
import functools
import math

import jax
import jax.numpy as jnp
from jax import lax
from jax.experimental import pallas as pl
from jax.experimental.pallas import tpu as pltpu
from jax.sharding import PartitionSpec as P

HEADS = 12
HD = 128
POS = 256
SPAN = 4
NWIN = 8
LOOK = 2
QB = 256
PARTS = HEADS // SPAN
POSITIONS = POS // NWIN
STAT_ROWS = 32
LOG2E = math.log2(math.e)
FACTOR = HD**-0.5 * LOG2E
NEG_FILL = -1e30
SMEM = pl.BlockSpec(memory_space=pltpu.SMEM)
VMEM = pl.BlockSpec(memory_space=pltpu.VMEM)
ANY = pl.BlockSpec(memory_space=pl.ANY)
HBM = pl.BlockSpec(memory_space=pltpu.HBM)
SMALL = pltpu.CompilerParams(vmem_limit_bytes=2**20)
PARAMS = pltpu.CompilerParams(vmem_limit_bytes=8 * 2**20)


def is_taken(groups_ref, count_ref, group, distance):
    groups = groups_ref.shape[0]
    window = lax.axis_index("ctx") // SPAN
    held = jnp.minimum(group, groups - 1)
    source = group - distance
    count = count_ref[held, window]
    taken = jnp.bool_(False)
    for slot in range(LOOK):
        taken = taken | ((groups_ref[held, window, slot] == source) & (slot < count))
    return taken & (source >= 0) & (group < groups)


def flags_kernel(groups_ref, count_ref, out_ref):
    group = lax.axis_index("grp")
    for at, (owner, distance) in enumerate(((group, 1), (group, 2), (group + 1, 2))):
        out_ref[at] = is_taken(groups_ref, count_ref, owner, distance).astype(jnp.int32)
    out_ref[3] = jnp.int32(0)


def make_flags(groups, count):
    return pl.pallas_call(
        flags_kernel,
        in_specs=[SMEM] * 2,
        out_specs=SMEM,
        out_shape=jax.ShapeDtypeStruct((4,), jnp.int32),
        compiler_params=SMALL,
        name="flags",
    )(groups, count)


def score(query, keys):
    return lax.dot_general(
        query, keys, (((1,), (1,)), ((), ())), preferred_element_type=jnp.float32
    )


def soften(scores, values, diagonal=False):
    if diagonal:
        rows, count = scores.shape
        tail = scores[:, count - rows :]
        frame_query = lax.broadcasted_iota(jnp.int32, (rows, rows), 0) // POSITIONS
        frame_key = lax.broadcasted_iota(jnp.int32, (rows, rows), 1) // POSITIONS
        tail = jnp.where(frame_query >= frame_key, tail, NEG_FILL)
        scores = jnp.concatenate([scores[:, : count - rows], tail], axis=1) if count > rows else tail
    highest = jnp.max(scores, axis=-1, keepdims=True)
    weights = jnp.exp2((scores - highest) * FACTOR)
    summed = jnp.sum(weights, axis=-1, keepdims=True)
    blended = jnp.dot(weights.astype(jnp.bfloat16), values, preferred_element_type=jnp.float32)
    return highest, summed, blended


def in_turn(jobs, done):
    scores = jobs[0][0]()
    for at, (_, finish) in enumerate(jobs):
        following = jobs[at + 1][0]() if at + 1 < len(jobs) else None
        done(at, finish(scores))
        scores = following


def join(old, new):
    ceiling = jnp.maximum(old[0], new[0])
    old_scale = jnp.exp2((old[0] - ceiling) * FACTOR)
    new_scale = jnp.exp2((new[0] - ceiling) * FACTOR)
    return (
        ceiling,
        old[1] * old_scale + new[1] * new_scale,
        old[2] * old_scale + new[2] * new_scale,
    )


def rows_of(ref, slab, start, size):
    first, count = start // POSITIONS, size // POSITIONS
    return ref[pl.ds(first, count), slab].reshape(size, HD)


def eye_mask():
    return lax.broadcasted_iota(jnp.int32, (HD, HD), 0) == lax.broadcasted_iota(
        jnp.int32, (HD, HD), 1
    )


def log_rows(part):
    log_sum = part[0] * FACTOR + jnp.log(part[1]) * LOG2E
    return [
        jnp.sum(jnp.where(eye_mask(), log_sum[at : at + HD], 0.0), axis=0, keepdims=True)
        for at in range(0, log_sum.shape[0], HD)
    ]


def ahead_kernel(flags_ref, q_ref, kv_ref, out_ref):
    rows = q_ref.shape[0] * POSITIONS
    heads = out_ref.shape[0]
    taken = flags_ref[2] > 0

    @pl.when(taken)
    def _():
        @pl.loop(0, heads)
        def _(head):
            keys = kv_ref[:, 2 * head].reshape(rows, HD)
            values = kv_ref[:, 2 * head + 1].reshape(rows, HD)

            def job(start):
                return (
                    lambda: score(rows_of(q_ref, head, start, QB), keys),
                    lambda scores: soften(scores, values),
                )

            logs = []

            def done(at, part):
                out_ref[head, pl.ds(at * QB, QB), :] = (part[2] / part[1]).astype(jnp.bfloat16)
                logs.extend(log_rows(part))

            in_turn([job(start) for start in range(0, rows, QB)], done)
            left = jnp.concatenate(logs, axis=0)
            pieces = []
            for _ in range(3):
                pieces.append(left.astype(jnp.bfloat16).astype(jnp.float32))
                left = left - pieces[-1]
            pieces.append(jnp.zeros((STAT_ROWS - 3 * left.shape[0], HD), jnp.float32))
            packed = jnp.concatenate(pieces, axis=0).astype(jnp.bfloat16)
            out_ref[head, pl.ds(rows, STAT_ROWS), :] = packed

    @pl.when(jnp.logical_not(taken))
    def _():
        out_ref[:, pl.ds(rows, STAT_ROWS), :] = jnp.zeros((heads, STAT_ROWS, HD), jnp.bfloat16)


def near_kernel(query_slab, flags_ref, q_ref, own_ref, up_ref, out_ref, log_ref):
    rows = q_ref.shape[0] * POSITIONS
    heads = out_ref.shape[0]
    taken = flags_ref[0] > 0

    def run(with_earlier):
        @pl.loop(0, heads)
        def _(head):
            def own(start):
                def begin():
                    query = rows_of(q_ref, query_slab + head, start, QB)
                    return score(query, rows_of(own_ref, 2 * head, 0, start + QB))

                def finish(scores):
                    return soften(scores, rows_of(own_ref, 2 * head + 1, 0, start + QB), True)

                return begin, finish

            def earlier(start):
                def begin():
                    query = rows_of(q_ref, query_slab + head, start, QB)
                    return score(query, rows_of(up_ref, 2 * head, 0, rows))

                def finish(scores):
                    return soften(scores, rows_of(up_ref, 2 * head + 1, 0, rows))

                return begin, finish

            logs = []
            held = []

            def done(at, part):
                if with_earlier:
                    held.append(part)
                    if at % 2 == 0:
                        return
                    part = join(held[-2], held[-1])
                    at = at // 2
                out_ref[head, pl.ds(at * QB, QB), :] = part[2] / part[1]
                logs.extend(log_rows(part))

            jobs = []
            for start in range(0, rows, QB):
                jobs.append(own(start))
                if with_earlier:
                    jobs.append(earlier(start))
            in_turn(jobs, done)
            log_ref[head] = jnp.concatenate(logs, axis=0)

    @pl.when(taken)
    def _():
        run(True)

    @pl.when(jnp.logical_not(taken))
    def _():
        run(False)


def merge_kernel(flags_ref, near_a, near_b, log_a, log_b, far_a, far_b, out_ref):
    rows = near_a.shape[1]
    blocks = rows // HD
    taken = flags_ref[1] > 0

    def put(head, block, value):
        count = HD // POSITIONS
        frames = pl.ds(block * count, count)
        out_ref[frames, head] = value.astype(jnp.bfloat16).reshape(count, POSITIONS, HD)

    def each_head():
        count = near_a.shape[0]
        for head in range(PARTS):
            refs = (near_a, log_a, far_a) if head < count else (near_b, log_b, far_b)
            yield (head,) + tuple(ref.at[head if head < count else head - count] for ref in refs)

    @pl.when(taken)
    def _():
        for head, near_ref, log_ref, far_ref in each_head():
            pieces = far_ref[pl.ds(rows, STAT_ROWS), :].astype(jnp.float32)
            far_log = pieces[:blocks] + pieces[blocks : 2 * blocks] + pieces[2 * blocks : 3 * blocks]
            shares = jnp.transpose(1.0 / (1.0 + jnp.exp2(log_ref[...] - far_log)))
            for block in range(blocks):
                part = pl.ds(block * HD, HD)
                near = near_ref[part, :]
                far = far_ref[part, :].astype(jnp.float32)
                put(head, block, near + (far - near) * shares[:, block : block + 1])

    @pl.when(jnp.logical_not(taken))
    def _():
        for head, near_ref, _, _ in each_head():
            for block in range(blocks):
                put(head, block, near_ref[pl.ds(block * HD, HD), :])


def cost(passes, rows, heads, moved):
    return pl.CostEstimate(
        flops=int(4 * passes * rows * rows * heads * HD),
        bytes_accessed=moved,
        transcendentals=int(passes * rows * rows * heads),
    )


def attend_ahead(flags, query, pair):
    rows, heads = pair.shape[0] * POSITIONS, pair.shape[1] // 2
    return pl.pallas_call(
        ahead_kernel,
        in_specs=[SMEM] + [VMEM] * 2,
        out_specs=VMEM,
        out_shape=jax.ShapeDtypeStruct((heads, rows + STAT_ROWS, HD), jnp.bfloat16),
        compiler_params=PARAMS,
        cost_estimate=cost(1, rows, heads, rows * heads * HD * 8),
        name="ahead",
    )(flags, query, pair)


def attend_near(flags, query, query_slab, own, pair):
    rows, heads = pair.shape[0] * POSITIONS, pair.shape[1] // 2
    return pl.pallas_call(
        functools.partial(near_kernel, query_slab),
        in_specs=[SMEM] + [VMEM] * 3,
        out_specs=[VMEM] * 2,
        out_shape=[
            jax.ShapeDtypeStruct((heads, rows, HD), jnp.float32),
            jax.ShapeDtypeStruct((heads, rows // HD, HD), jnp.float32),
        ],
        compiler_params=PARAMS,
        cost_estimate=cost(1.6, rows, heads, rows * heads * HD * 14),
        name="near",
    )(flags, query, own, pair)


def merge(flags, near, logs, far):
    rows = near[0].shape[1]
    return pl.pallas_call(
        merge_kernel,
        in_specs=[SMEM] + [VMEM] * 6,
        out_specs=VMEM,
        out_shape=jax.ShapeDtypeStruct((rows // POSITIONS, PARTS, POSITIONS, HD), jnp.bfloat16),
        compiler_params=PARAMS,
        cost_estimate=cost(0, rows, PARTS, rows * PARTS * HD * 8),
        name="merge",
    )(flags, *near, *logs, *far)


def cut_first_kernel(k_ref, v_ref, out_ref, held_ref, piece_ref, in_sems, out_sems):
    def fetch(which, window):
        rows = pl.ds(window * POSITIONS, POSITIONS)
        ref = (k_ref, v_ref)[which]
        return pltpu.make_async_copy(
            ref.at[rows], held_ref.at[which, rows], in_sems.at[which, window]
        )

    def store(window):
        peers = pl.ds(window * SPAN, SPAN)
        return pltpu.make_async_copy(piece_ref.at[peers], out_ref.at[peers], out_sems.at[window])

    for window in range(NWIN):
        for which in range(2):
            fetch(which, window).start()
    for window in range(NWIN):
        rows = pl.ds(window * POSITIONS, POSITIONS)
        for which in range(2):
            fetch(which, window).wait()
            for part in range(SPAN):
                for head in range(2):
                    lanes = pl.ds((part * PARTS + head) * HD, HD)
                    piece_ref[window * SPAN + part, 2 * head + which] = held_ref[which, rows, lanes]
        store(window).start()
    for window in range(NWIN):
        store(window).wait()


def cut_first(key, value):
    shape = (NWIN * SPAN, 4, POSITIONS, HD)
    return pl.pallas_call(
        cut_first_kernel,
        in_specs=[HBM] * 2,
        out_specs=HBM,
        out_shape=jax.ShapeDtypeStruct(shape, jnp.bfloat16),
        scratch_shapes=[
            pltpu.VMEM((2,) + key.shape, jnp.bfloat16),
            pltpu.VMEM(shape, jnp.bfloat16),
            pltpu.SemaphoreType.DMA((2, NWIN)),
            pltpu.SemaphoreType.DMA((NWIN,)),
        ],
        compiler_params=pltpu.CompilerParams(vmem_limit_bytes=60 * 2**20),
        name="cut_first",
    )(key, value)


def gate_kernel(*refs):
    del refs


def gate(passed, *waited):
    return pl.pallas_call(
        gate_kernel,
        in_specs=[ANY] * (1 + len(waited)),
        out_specs=ANY,
        out_shape=jax.ShapeDtypeStruct(passed.shape, passed.dtype),
        input_output_aliases={0: 0},
        compiler_params=SMALL,
        name="gate",
    )(passed, *waited)


def cut_kernel(slabs, *refs):
    sources, out_ref = refs[:-1], refs[-1]
    for window in range(NWIN):
        rows = pl.ds(window * POSITIONS, POSITIONS)
        for part in range(SPAN):
            for slab, (source, head) in enumerate(slabs):
                lanes = pl.ds((part * PARTS + head) * HD, HD)
                out_ref[window * SPAN + part, slab] = sources[source][rows, lanes]


def cut(sources, slabs):
    return pl.pallas_call(
        functools.partial(cut_kernel, slabs),
        in_specs=[VMEM] * len(sources),
        out_specs=VMEM,
        out_shape=jax.ShapeDtypeStruct((NWIN * SPAN, len(slabs), POSITIONS, HD), jnp.bfloat16),
        compiler_params=PARAMS,
        cost_estimate=pl.CostEstimate(flops=10**11, bytes_accessed=2**22, transcendentals=0),
        name="cut",
    )(*sources)


def paste_kernel(in_ref, out_ref, held_ref, sems):
    copies = []
    for window in range(NWIN):
        rows = pl.ds(window * POSITIONS, POSITIONS)
        for part in range(SPAN):
            for head in range(PARTS):
                lanes = pl.ds((part * PARTS + head) * HD, HD)
                held_ref[rows, lanes] = in_ref[window * SPAN + part, head]
        copies.append(
            pltpu.make_async_copy(held_ref.at[rows], out_ref.at[rows], sems.at[window])
        )
        copies[-1].start()
    for copy in copies:
        copy.wait()


def paste(pieces):
    return pl.pallas_call(
        paste_kernel,
        in_specs=[VMEM],
        out_specs=ANY,
        out_shape=jax.ShapeDtypeStruct((POS, HEADS * HD), jnp.bfloat16),
        scratch_shapes=[
            pltpu.VMEM((POS, HEADS * HD), jnp.bfloat16),
            pltpu.SemaphoreType.DMA((NWIN,)),
        ],
        compiler_params=PARAMS,
        name="paste",
    )(pieces)


def body(query_vectors, key_vectors, value_vectors, chosen_groups, chosen_count):
    group_devices = lax.axis_size("grp")

    def to_peers(block):
        return lax.all_to_all(block, "ctx", split_axis=0, concat_axis=0, tiled=True)

    def up(block):
        return lax.ppermute(block, "grp", [(at, at + 1) for at in range(group_devices - 1)])

    def down(block):
        return lax.ppermute(block, "grp", [(at + 1, at) for at in range(group_devices - 1)])

    later_query = down(query_vectors)
    first = to_peers(cut_first(key_vectors, value_vectors))
    first_up = up(first)
    flags = make_flags(chosen_groups, chosen_count)
    second = cut(
        (key_vectors, value_vectors, later_query), ((0, 2), (1, 2), (2, 0), (2, 1), (2, 2))
    )
    second = to_peers(gate(second, first, flags))
    second_pair = second[:, 0:2]
    second_up = up(second_pair)
    query = to_peers(gate(cut((query_vectors,), ((0, 0), (0, 1), (0, 2))), second_pair))
    first_far = up(attend_ahead(flags, second[:, 2:4], first_up))
    second_far = up(attend_ahead(flags, second[:, 4:5], second_up))
    near_a, log_a = attend_near(flags, query, 0, first, first_up)
    near_b, log_b = attend_near(flags, query, 2, second_pair, second_up)
    merged = merge(flags, (near_a, near_b), (log_a, log_b), (first_far, second_far))
    return paste(to_peers(merged))


def solution(mesh):
    in_specs = (P(("grp", "ctx"), None), P(("grp", "ctx"), None), P(("grp", "ctx"), None), P(), P())
    out_specs = P(("grp", "ctx"), None)
    return jax.shard_map(body, mesh=mesh, in_specs=in_specs, out_specs=out_specs, check_vma=False)
```

```python
import functools
import math

import jax
import jax.numpy as jnp
from jax import lax
from jax.experimental import pallas as pl
from jax.experimental.pallas import tpu as pltpu
from jax.sharding import PartitionSpec as P

HEADS = 12
HD = 128
POS = 256
SPAN = 4
NWIN = 8
LOOK = 2
QB = 256
PARTS = HEADS // SPAN
POSITIONS = POS // NWIN
STAT_ROWS = 32
LOG2E = math.log2(math.e)
FACTOR = HD**-0.5 * LOG2E
NEG_FILL = -1e30
SMEM = pl.BlockSpec(memory_space=pltpu.SMEM)
VMEM = pl.BlockSpec(memory_space=pltpu.VMEM)
ANY = pl.BlockSpec(memory_space=pl.ANY)
HBM = pl.BlockSpec(memory_space=pltpu.HBM)
SMALL = pltpu.CompilerParams(vmem_limit_bytes=2**20)
PARAMS = pltpu.CompilerParams(vmem_limit_bytes=8 * 2**20)


def is_taken(groups_ref, count_ref, group, distance):
    groups = groups_ref.shape[0]
    window = lax.axis_index("ctx") // SPAN
    held = jnp.minimum(group, groups - 1)
    source = group - distance
    count = count_ref[held, window]
    taken = jnp.bool_(False)
    for slot in range(LOOK):
        taken = taken | ((groups_ref[held, window, slot] == source) & (slot < count))
    return taken & (source >= 0) & (group < groups)


def flags_kernel(groups_ref, count_ref, out_ref):
    group = lax.axis_index("grp")
    for at, (owner, distance) in enumerate(((group, 1), (group, 2), (group + 1, 2))):
        out_ref[at] = is_taken(groups_ref, count_ref, owner, distance).astype(jnp.int32)
    out_ref[3] = jnp.int32(0)


def make_flags(groups, count):
    return pl.pallas_call(
        flags_kernel,
        in_specs=[SMEM] * 2,
        out_specs=SMEM,
        out_shape=jax.ShapeDtypeStruct((4,), jnp.int32),
        compiler_params=SMALL,
        name="flags",
    )(groups, count)


def score(query, keys):
    return lax.dot_general(
        query, keys, (((1,), (1,)), ((), ())), preferred_element_type=jnp.float32
    )


def soften(scores, values, diagonal=False):
    if diagonal:
        rows, count = scores.shape
        tail = scores[:, count - rows :]
        frame_query = lax.broadcasted_iota(jnp.int32, (rows, rows), 0) // POSITIONS
        frame_key = lax.broadcasted_iota(jnp.int32, (rows, rows), 1) // POSITIONS
        tail = jnp.where(frame_query >= frame_key, tail, NEG_FILL)
        scores = jnp.concatenate([scores[:, : count - rows], tail], axis=1) if count > rows else tail
    highest = jnp.max(scores, axis=-1, keepdims=True)
    weights = jnp.exp2((scores - highest) * FACTOR)
    summed = jnp.sum(weights, axis=-1, keepdims=True)
    blended = jnp.dot(weights.astype(jnp.bfloat16), values, preferred_element_type=jnp.float32)
    return highest, summed, blended


def in_turn(jobs, done):
    scores = jobs[0][0]()
    for at, (_, finish) in enumerate(jobs):
        following = jobs[at + 1][0]() if at + 1 < len(jobs) else None
        done(at, finish(scores))
        scores = following


def join(old, new):
    ceiling = jnp.maximum(old[0], new[0])
    old_scale = jnp.exp2((old[0] - ceiling) * FACTOR)
    new_scale = jnp.exp2((new[0] - ceiling) * FACTOR)
    return (
        ceiling,
        old[1] * old_scale + new[1] * new_scale,
        old[2] * old_scale + new[2] * new_scale,
    )


def rows_of(ref, slab, start, size):
    first, count = start // POSITIONS, size // POSITIONS
    return ref[pl.ds(first, count), slab].reshape(size, HD)


def eye_mask():
    return lax.broadcasted_iota(jnp.int32, (HD, HD), 0) == lax.broadcasted_iota(
        jnp.int32, (HD, HD), 1
    )


def log_rows(part):
    log_sum = part[0] * FACTOR + jnp.log(part[1]) * LOG2E
    return [
        jnp.sum(jnp.where(eye_mask(), log_sum[at : at + HD], 0.0), axis=0, keepdims=True)
        for at in range(0, log_sum.shape[0], HD)
    ]


def ahead_kernel(flags_ref, q_ref, kv_ref, out_ref):
    rows = q_ref.shape[0] * POSITIONS
    heads = out_ref.shape[0]
    taken = flags_ref[2] > 0

    @pl.when(taken)
    def _():
        @pl.loop(0, heads)
        def _(head):
            keys = kv_ref[:, 2 * head].reshape(rows, HD)
            values = kv_ref[:, 2 * head + 1].reshape(rows, HD)

            def job(start):
                return (
                    lambda: score(rows_of(q_ref, head, start, QB), keys),
                    lambda scores: soften(scores, values),
                )

            logs = []

            def done(at, part):
                out_ref[head, pl.ds(at * QB, QB), :] = (part[2] / part[1]).astype(jnp.bfloat16)
                logs.extend(log_rows(part))

            in_turn([job(start) for start in range(0, rows, QB)], done)
            left = jnp.concatenate(logs, axis=0)
            pieces = []
            for _ in range(3):
                pieces.append(left.astype(jnp.bfloat16).astype(jnp.float32))
                left = left - pieces[-1]
            pieces.append(jnp.zeros((STAT_ROWS - 3 * left.shape[0], HD), jnp.float32))
            packed = jnp.concatenate(pieces, axis=0).astype(jnp.bfloat16)
            out_ref[head, pl.ds(rows, STAT_ROWS), :] = packed

    @pl.when(jnp.logical_not(taken))
    def _():
        out_ref[:, pl.ds(rows, STAT_ROWS), :] = jnp.zeros((heads, STAT_ROWS, HD), jnp.bfloat16)


def near_kernel(query_slab, flags_ref, q_ref, own_ref, up_ref, out_ref, log_ref):
    rows = q_ref.shape[0] * POSITIONS
    heads = out_ref.shape[0]
    taken = flags_ref[0] > 0

    def run(with_earlier):
        @pl.loop(0, heads)
        def _(head):
            def own(start):
                def begin():
                    query = rows_of(q_ref, query_slab + head, start, QB)
                    return score(query, rows_of(own_ref, 2 * head, 0, start + QB))

                def finish(scores):
                    return soften(scores, rows_of(own_ref, 2 * head + 1, 0, start + QB), True)

                return begin, finish

            def earlier(start):
                def begin():
                    query = rows_of(q_ref, query_slab + head, start, QB)
                    return score(query, rows_of(up_ref, 2 * head, 0, rows))

                def finish(scores):
                    return soften(scores, rows_of(up_ref, 2 * head + 1, 0, rows))

                return begin, finish

            logs = []
            held = []

            def done(at, part):
                if with_earlier:
                    held.append(part)
                    if at % 2 == 0:
                        return
                    part = join(held[-2], held[-1])
                    at = at // 2
                out_ref[head, pl.ds(at * QB, QB), :] = part[2] / part[1]
                logs.extend(log_rows(part))

            jobs = []
            for start in range(0, rows, QB):
                jobs.append(own(start))
                if with_earlier:
                    jobs.append(earlier(start))
            in_turn(jobs, done)
            log_ref[head] = jnp.concatenate(logs, axis=0)

    @pl.when(taken)
    def _():
        run(True)

    @pl.when(jnp.logical_not(taken))
    def _():
        run(False)


def merge_kernel(flags_ref, near_a, near_b, log_a, log_b, far_a, far_b, out_ref):
    rows = near_a.shape[1]
    blocks = rows // HD
    taken = flags_ref[1] > 0

    def put(head, block, value):
        count = HD // POSITIONS
        frames = pl.ds(block * count, count)
        out_ref[frames, head] = value.astype(jnp.bfloat16).reshape(count, POSITIONS, HD)

    def each_head():
        count = near_a.shape[0]
        for head in range(PARTS):
            refs = (near_a, log_a, far_a) if head < count else (near_b, log_b, far_b)
            yield (head,) + tuple(ref.at[head if head < count else head - count] for ref in refs)

    @pl.when(taken)
    def _():
        for head, near_ref, log_ref, far_ref in each_head():
            pieces = far_ref[pl.ds(rows, STAT_ROWS), :].astype(jnp.float32)
            far_log = pieces[:blocks] + pieces[blocks : 2 * blocks] + pieces[2 * blocks : 3 * blocks]
            shares = jnp.transpose(1.0 / (1.0 + jnp.exp2(log_ref[...] - far_log)))
            for block in range(blocks):
                part = pl.ds(block * HD, HD)
                near = near_ref[part, :]
                far = far_ref[part, :].astype(jnp.float32)
                put(head, block, near + (far - near) * shares[:, block : block + 1])

    @pl.when(jnp.logical_not(taken))
    def _():
        for head, near_ref, _, _ in each_head():
            for block in range(blocks):
                put(head, block, near_ref[pl.ds(block * HD, HD), :])


def cost(passes, rows, heads, moved):
    return pl.CostEstimate(
        flops=int(4 * passes * rows * rows * heads * HD),
        bytes_accessed=moved,
        transcendentals=int(passes * rows * rows * heads),
    )


def attend_ahead(flags, query, pair, flops):
    rows, heads = pair.shape[0] * POSITIONS, pair.shape[1] // 2
    return pl.pallas_call(
        ahead_kernel,
        in_specs=[SMEM] + [VMEM] * 2,
        out_specs=VMEM,
        out_shape=jax.ShapeDtypeStruct((heads, rows + STAT_ROWS, HD), jnp.bfloat16),
        compiler_params=PARAMS,
        cost_estimate=pl.CostEstimate(flops=flops, bytes_accessed=2**20, transcendentals=0),
        name="ahead",
    )(flags, query, pair)


def attend_near(flags, query, query_slab, own, pair):
    rows, heads = pair.shape[0] * POSITIONS, pair.shape[1] // 2
    return pl.pallas_call(
        functools.partial(near_kernel, query_slab),
        in_specs=[SMEM] + [VMEM] * 3,
        out_specs=[VMEM] * 2,
        out_shape=[
            jax.ShapeDtypeStruct((heads, rows, HD), jnp.float32),
            jax.ShapeDtypeStruct((heads, rows // HD, HD), jnp.float32),
        ],
        compiler_params=PARAMS,
        cost_estimate=cost(1.6, rows, heads, rows * heads * HD * 14),
        name="near",
    )(flags, query, own, pair)


def merge(flags, near, logs, far):
    rows = near[0].shape[1]
    return pl.pallas_call(
        merge_kernel,
        in_specs=[SMEM] + [VMEM] * 6,
        out_specs=VMEM,
        out_shape=jax.ShapeDtypeStruct((rows // POSITIONS, PARTS, POSITIONS, HD), jnp.bfloat16),
        compiler_params=PARAMS,
        cost_estimate=cost(0, rows, PARTS, rows * PARTS * HD * 8),
        name="merge",
    )(flags, *near, *logs, *far)


def cut_first_kernel(k_ref, v_ref, out_ref, held_ref, piece_ref, in_sems, out_sems):
    def fetch(which, window):
        rows = pl.ds(window * POSITIONS, POSITIONS)
        ref = (k_ref, v_ref)[which]
        return pltpu.make_async_copy(
            ref.at[rows], held_ref.at[which, rows], in_sems.at[which, window]
        )

    def store(window):
        peers = pl.ds(window * SPAN, SPAN)
        return pltpu.make_async_copy(piece_ref.at[peers], out_ref.at[peers], out_sems.at[window])

    for window in range(NWIN):
        for which in range(2):
            fetch(which, window).start()
    for window in range(NWIN):
        rows = pl.ds(window * POSITIONS, POSITIONS)
        for which in range(2):
            fetch(which, window).wait()
            for part in range(SPAN):
                for head in range(2):
                    lanes = pl.ds((part * PARTS + head) * HD, HD)
                    piece_ref[window * SPAN + part, 2 * head + which] = held_ref[which, rows, lanes]
        store(window).start()
    for window in range(NWIN):
        store(window).wait()


def cut_first(key, value):
    shape = (NWIN * SPAN, 4, POSITIONS, HD)
    return pl.pallas_call(
        cut_first_kernel,
        in_specs=[HBM] * 2,
        out_specs=HBM,
        out_shape=jax.ShapeDtypeStruct(shape, jnp.bfloat16),
        scratch_shapes=[
            pltpu.VMEM((2,) + key.shape, jnp.bfloat16),
            pltpu.VMEM(shape, jnp.bfloat16),
            pltpu.SemaphoreType.DMA((2, NWIN)),
            pltpu.SemaphoreType.DMA((NWIN,)),
        ],
        compiler_params=pltpu.CompilerParams(vmem_limit_bytes=60 * 2**20),
        name="cut_first",
    )(key, value)


def gate_kernel(*refs):
    del refs


def gate(passed, *waited):
    return pl.pallas_call(
        gate_kernel,
        in_specs=[ANY] * (1 + len(waited)),
        out_specs=ANY,
        out_shape=jax.ShapeDtypeStruct(passed.shape, passed.dtype),
        input_output_aliases={0: 0},
        compiler_params=SMALL,
        name="gate",
    )(passed, *waited)


def cut_kernel(slabs, *refs):
    sources, out_ref = refs[:-1], refs[-1]
    for window in range(NWIN):
        rows = pl.ds(window * POSITIONS, POSITIONS)
        for part in range(SPAN):
            for slab, (source, head) in enumerate(slabs):
                lanes = pl.ds((part * PARTS + head) * HD, HD)
                out_ref[window * SPAN + part, slab] = sources[source][rows, lanes]


def cut(sources, slabs, flops):
    return pl.pallas_call(
        functools.partial(cut_kernel, slabs),
        in_specs=[VMEM] * len(sources),
        out_specs=VMEM,
        out_shape=jax.ShapeDtypeStruct((NWIN * SPAN, len(slabs), POSITIONS, HD), jnp.bfloat16),
        compiler_params=PARAMS,
        cost_estimate=pl.CostEstimate(flops=flops, bytes_accessed=2**21, transcendentals=0),
        name="cut",
    )(*sources)


def paste_kernel(in_ref, out_ref, held_ref, sems):
    copies = []
    for window in range(NWIN):
        rows = pl.ds(window * POSITIONS, POSITIONS)
        for part in range(SPAN):
            for head in range(PARTS):
                lanes = pl.ds((part * PARTS + head) * HD, HD)
                held_ref[rows, lanes] = in_ref[window * SPAN + part, head]
        copies.append(
            pltpu.make_async_copy(held_ref.at[rows], out_ref.at[rows], sems.at[window])
        )
        copies[-1].start()
    for copy in copies:
        copy.wait()


def paste(pieces):
    return pl.pallas_call(
        paste_kernel,
        in_specs=[VMEM],
        out_specs=ANY,
        out_shape=jax.ShapeDtypeStruct((POS, HEADS * HD), jnp.bfloat16),
        scratch_shapes=[
            pltpu.VMEM((POS, HEADS * HD), jnp.bfloat16),
            pltpu.SemaphoreType.DMA((NWIN,)),
        ],
        compiler_params=PARAMS,
        name="paste",
    )(pieces)


def body(query_vectors, key_vectors, value_vectors, chosen_groups, chosen_count):
    group_devices = lax.axis_size("grp")

    def to_peers(block):
        return lax.all_to_all(block, "ctx", split_axis=0, concat_axis=0, tiled=True)

    def up(block):
        return lax.ppermute(block, "grp", [(at, at + 1) for at in range(group_devices - 1)])

    def down(block):
        return lax.ppermute(block, "grp", [(at + 1, at) for at in range(group_devices - 1)])

    later_query = down(query_vectors)
    first = to_peers(cut_first(key_vectors, value_vectors))
    first_up = up(first)
    flags = make_flags(chosen_groups, chosen_count)
    second = cut(
        (key_vectors, value_vectors, later_query), ((0, 2), (1, 2), (2, 0), (2, 1)), 10**11
    )
    third = cut((query_vectors, later_query), ((0, 0), (0, 1), (0, 2), (1, 2)), 10**6)
    second = to_peers(gate(second, first, flags))
    second_pair = second[:, 0:2]
    second_up = up(second_pair)
    third = to_peers(gate(third, second_pair))
    first_far = up(attend_ahead(flags, second[:, 2:4], first_up, 10**6))
    second_far = up(attend_ahead(flags, third[:, 3:4], second_up, 10**11))
    near_a, log_a = attend_near(flags, third, 0, first, first_up)
    near_b, log_b = attend_near(flags, third, 2, second_pair, second_up)
    merged = merge(flags, (near_a, near_b), (log_a, log_b), (first_far, second_far))
    return paste(to_peers(merged))


def solution(mesh):
    in_specs = (P(("grp", "ctx"), None), P(("grp", "ctx"), None), P(("grp", "ctx"), None), P(), P())
    out_specs = P(("grp", "ctx"), None)
    return jax.shard_map(body, mesh=mesh, in_specs=in_specs, out_specs=out_specs, check_vma=False)
```

```python
import functools
import math

import jax
import jax.numpy as jnp
from jax import lax
from jax.experimental import pallas as pl
from jax.experimental.pallas import tpu as pltpu
from jax.sharding import PartitionSpec as P

HEADS = 12
HD = 128
POS = 256
SPAN = 4
NWIN = 8
LOOK = 2
QB = 256
PARTS = HEADS // SPAN
POSITIONS = POS // NWIN
STAT_ROWS = 32
LOG2E = math.log2(math.e)
FACTOR = HD**-0.5 * LOG2E
NEG_FILL = -1e30
SMEM = pl.BlockSpec(memory_space=pltpu.SMEM)
VMEM = pl.BlockSpec(memory_space=pltpu.VMEM)
ANY = pl.BlockSpec(memory_space=pl.ANY)
HBM = pl.BlockSpec(memory_space=pltpu.HBM)
SMALL = pltpu.CompilerParams(vmem_limit_bytes=2**20)
PARAMS = pltpu.CompilerParams(vmem_limit_bytes=8 * 2**20)


def is_taken(groups_ref, count_ref, group, distance):
    groups = groups_ref.shape[0]
    window = lax.axis_index("ctx") // SPAN
    held = jnp.minimum(group, groups - 1)
    source = group - distance
    count = count_ref[held, window]
    taken = jnp.bool_(False)
    for slot in range(LOOK):
        taken = taken | ((groups_ref[held, window, slot] == source) & (slot < count))
    return taken & (source >= 0) & (group < groups)


def flags_kernel(groups_ref, count_ref, out_ref):
    group = lax.axis_index("grp")
    for at, (owner, distance) in enumerate(((group, 1), (group, 2), (group + 1, 2))):
        out_ref[at] = is_taken(groups_ref, count_ref, owner, distance).astype(jnp.int32)
    out_ref[3] = jnp.int32(0)


def make_flags(groups, count):
    return pl.pallas_call(
        flags_kernel,
        in_specs=[SMEM] * 2,
        out_specs=SMEM,
        out_shape=jax.ShapeDtypeStruct((4,), jnp.int32),
        compiler_params=SMALL,
        name="flags",
    )(groups, count)


def score(query, keys):
    return lax.dot_general(
        query, keys, (((1,), (1,)), ((), ())), preferred_element_type=jnp.float32
    )


def soften(scores, values, diagonal=False):
    if diagonal:
        rows, count = scores.shape
        tail = scores[:, count - rows :]
        frame_query = lax.broadcasted_iota(jnp.int32, (rows, rows), 0) // POSITIONS
        frame_key = lax.broadcasted_iota(jnp.int32, (rows, rows), 1) // POSITIONS
        tail = jnp.where(frame_query >= frame_key, tail, NEG_FILL)
        scores = jnp.concatenate([scores[:, : count - rows], tail], axis=1) if count > rows else tail
    highest = jnp.max(scores, axis=-1, keepdims=True)
    weights = jnp.exp2((scores - highest) * FACTOR)
    beside = jnp.concatenate([values, jnp.ones_like(values)], axis=1)
    product = jnp.dot(weights.astype(jnp.bfloat16), beside, preferred_element_type=jnp.float32)
    return highest, product[:, HD:], product[:, :HD]


def in_turn(jobs, done):
    scores = jobs[0][0]()
    for at, (_, finish) in enumerate(jobs):
        following = jobs[at + 1][0]() if at + 1 < len(jobs) else None
        done(at, finish(scores))
        scores = following


def join(old, new):
    ceiling = jnp.maximum(old[0], new[0])
    old_scale = jnp.exp2((old[0] - ceiling) * FACTOR)
    new_scale = jnp.exp2((new[0] - ceiling) * FACTOR)
    return (
        ceiling,
        old[1] * old_scale + new[1] * new_scale,
        old[2] * old_scale + new[2] * new_scale,
    )


def rows_of(ref, slab, start, size):
    first, count = start // POSITIONS, size // POSITIONS
    return ref[pl.ds(first, count), slab].reshape(size, HD)


def eye_mask():
    return lax.broadcasted_iota(jnp.int32, (HD, HD), 0) == lax.broadcasted_iota(
        jnp.int32, (HD, HD), 1
    )


def log_rows(part):
    log_sum = part[0] * FACTOR + jnp.log(part[1]) * LOG2E
    return [
        jnp.sum(jnp.where(eye_mask(), log_sum[at : at + HD], 0.0), axis=0, keepdims=True)
        for at in range(0, log_sum.shape[0], HD)
    ]


def ahead_kernel(query_slab, pair_slab, flags_ref, q_ref, kv_ref, *rest):
    out_ref = rest[-1]
    rows = q_ref.shape[0] * POSITIONS
    heads = out_ref.shape[0]
    taken = flags_ref[2] > 0

    @pl.when(taken)
    def _():
        @pl.loop(0, heads)
        def _(head):
            keys = kv_ref[:, pair_slab + 2 * head].reshape(rows, HD)
            values = kv_ref[:, pair_slab + 2 * head + 1].reshape(rows, HD)

            def job(start):
                return (
                    lambda: score(rows_of(q_ref, query_slab + head, start, QB), keys),
                    lambda scores: soften(scores, values),
                )

            logs = []

            def done(at, part):
                out_ref[head, pl.ds(at * QB, QB), :] = (part[2] / part[1]).astype(jnp.bfloat16)
                logs.extend(log_rows(part))

            in_turn([job(start) for start in range(0, rows, QB)], done)
            left = jnp.concatenate(logs, axis=0)
            pieces = []
            for _ in range(3):
                pieces.append(left.astype(jnp.bfloat16).astype(jnp.float32))
                left = left - pieces[-1]
            pieces.append(jnp.zeros((STAT_ROWS - 3 * left.shape[0], HD), jnp.float32))
            packed = jnp.concatenate(pieces, axis=0).astype(jnp.bfloat16)
            out_ref[head, pl.ds(rows, STAT_ROWS), :] = packed

    @pl.when(jnp.logical_not(taken))
    def _():
        out_ref[:, pl.ds(rows, STAT_ROWS), :] = jnp.zeros((heads, STAT_ROWS, HD), jnp.bfloat16)


def near_kernel(query_slab, own_slab, up_slab, flags_ref, q_ref, own_ref, up_ref, out_ref, log_ref):
    rows = q_ref.shape[0] * POSITIONS
    heads = out_ref.shape[0]
    taken = flags_ref[0] > 0

    def run(with_earlier):
        @pl.loop(0, heads)
        def _(head):
            def own(start):
                def begin():
                    query = rows_of(q_ref, query_slab + head, start, QB)
                    return score(query, rows_of(own_ref, own_slab + 2 * head, 0, start + QB))

                def finish(scores):
                    return soften(scores, rows_of(own_ref, own_slab + 2 * head + 1, 0, start + QB), True)

                return begin, finish

            def earlier(start):
                def begin():
                    query = rows_of(q_ref, query_slab + head, start, QB)
                    return score(query, rows_of(up_ref, up_slab + 2 * head, 0, rows))

                def finish(scores):
                    return soften(scores, rows_of(up_ref, up_slab + 2 * head + 1, 0, rows))

                return begin, finish

            logs = []
            held = []

            def done(at, part):
                if with_earlier:
                    held.append(part)
                    if at % 2 == 0:
                        return
                    part = join(held[-2], held[-1])
                    at = at // 2
                out_ref[head, pl.ds(at * QB, QB), :] = part[2] / part[1]
                logs.extend(log_rows(part))

            jobs = []
            for start in range(0, rows, QB):
                jobs.append(own(start))
                if with_earlier:
                    jobs.append(earlier(start))
            in_turn(jobs, done)
            log_ref[head] = jnp.concatenate(logs, axis=0)

    @pl.when(taken)
    def _():
        run(True)

    @pl.when(jnp.logical_not(taken))
    def _():
        run(False)


def merge_kernel(flags_ref, near_a, near_b, log_a, log_b, far_a, far_b, out_ref):
    rows = near_a.shape[1]
    blocks = rows // HD
    taken = flags_ref[1] > 0

    def put(head, block, value):
        count = HD // POSITIONS
        frames = pl.ds(block * count, count)
        out_ref[frames, head] = value.astype(jnp.bfloat16).reshape(count, POSITIONS, HD)

    def each_head():
        count = near_a.shape[0]
        for head in range(PARTS):
            refs = (near_a, log_a, far_a) if head < count else (near_b, log_b, far_b)
            yield (head,) + tuple(ref.at[head if head < count else head - count] for ref in refs)

    @pl.when(taken)
    def _():
        for head, near_ref, log_ref, far_ref in each_head():
            pieces = far_ref[pl.ds(rows, STAT_ROWS), :].astype(jnp.float32)
            far_log = pieces[:blocks] + pieces[blocks : 2 * blocks] + pieces[2 * blocks : 3 * blocks]
            shares = jnp.transpose(1.0 / (1.0 + jnp.exp2(log_ref[...] - far_log)))
            for block in range(blocks):
                part = pl.ds(block * HD, HD)
                near = near_ref[part, :]
                far = far_ref[part, :].astype(jnp.float32)
                put(head, block, near + (far - near) * shares[:, block : block + 1])

    @pl.when(jnp.logical_not(taken))
    def _():
        for head, near_ref, _, _ in each_head():
            for block in range(blocks):
                put(head, block, near_ref[pl.ds(block * HD, HD), :])


def cost(passes, rows, heads, moved):
    return pl.CostEstimate(
        flops=int(4 * passes * rows * rows * heads * HD),
        bytes_accessed=moved,
        transcendentals=int(passes * rows * rows * heads),
    )


def attend_ahead(flags, heads, query, query_slab, pair, pair_slab, *waited):
    rows = pair.shape[0] * POSITIONS
    return pl.pallas_call(
        functools.partial(ahead_kernel, query_slab, pair_slab),
        in_specs=[SMEM] + [VMEM] * 2 + [ANY] * len(waited),
        out_specs=VMEM,
        out_shape=jax.ShapeDtypeStruct((heads, rows + STAT_ROWS, HD), jnp.bfloat16),
        compiler_params=PARAMS,
        cost_estimate=cost(1, rows, heads, rows * heads * HD * 8),
        name="ahead",
    )(flags, query, pair, *waited)


def attend_near(flags, heads, query, query_slab, own, own_slab, up, up_slab):
    rows = query.shape[0] * POSITIONS
    return pl.pallas_call(
        functools.partial(near_kernel, query_slab, own_slab, up_slab),
        in_specs=[SMEM] + [VMEM] * 3,
        out_specs=[VMEM] * 2,
        out_shape=[
            jax.ShapeDtypeStruct((heads, rows, HD), jnp.float32),
            jax.ShapeDtypeStruct((heads, rows // HD, HD), jnp.float32),
        ],
        compiler_params=PARAMS,
        cost_estimate=cost(1.6, rows, heads, rows * heads * HD * 14),
        name="near",
    )(flags, query, own, up)


def merge(flags, near, logs, far):
    rows = near[0].shape[1]
    return pl.pallas_call(
        merge_kernel,
        in_specs=[SMEM] + [VMEM] * 6,
        out_specs=VMEM,
        out_shape=jax.ShapeDtypeStruct((rows // POSITIONS, PARTS, POSITIONS, HD), jnp.bfloat16),
        compiler_params=PARAMS,
        cost_estimate=cost(0, rows, PARTS, rows * PARTS * HD * 8),
        name="merge",
    )(flags, *near, *logs, *far)


def cut_first_kernel(k_ref, v_ref, first_ref, last_ref, held_ref, first_piece, last_piece, *sems):
    in_sems, first_sems, last_sems = sems

    def fetch(which, window):
        rows = pl.ds(window * POSITIONS, POSITIONS)
        ref = (k_ref, v_ref)[which]
        return pltpu.make_async_copy(
            ref.at[rows], held_ref.at[which, rows], in_sems.at[which, window]
        )

    def stores(window):
        peers = pl.ds(window * SPAN, SPAN)
        return (
            pltpu.make_async_copy(first_piece.at[peers], first_ref.at[peers], first_sems.at[window]),
            pltpu.make_async_copy(last_piece.at[peers], last_ref.at[peers], last_sems.at[window]),
        )

    for window in range(NWIN):
        for which in range(2):
            fetch(which, window).start()
    for window in range(NWIN):
        rows = pl.ds(window * POSITIONS, POSITIONS)
        for which in range(2):
            fetch(which, window).wait()
            for part in range(SPAN):
                for head in range(PARTS):
                    lanes = pl.ds((part * PARTS + head) * HD, HD)
                    value = held_ref[which, rows, lanes]
                    if head < 2:
                        first_piece[window * SPAN + part, 2 * head + which] = value
                    else:
                        last_piece[window * SPAN + part, which] = value
        for copy in stores(window):
            copy.start()
    for window in range(NWIN):
        for copy in stores(window):
            copy.wait()


def cut_first(key, value):
    first = (NWIN * SPAN, 4, POSITIONS, HD)
    last = (NWIN * SPAN, 2, POSITIONS, HD)
    return pl.pallas_call(
        cut_first_kernel,
        in_specs=[HBM] * 2,
        out_specs=[HBM] * 2,
        out_shape=[jax.ShapeDtypeStruct(shape, jnp.bfloat16) for shape in (first, last)],
        scratch_shapes=[
            pltpu.VMEM((2,) + key.shape, jnp.bfloat16),
            pltpu.VMEM(first, jnp.bfloat16),
            pltpu.VMEM(last, jnp.bfloat16),
            pltpu.SemaphoreType.DMA((2, NWIN)),
            pltpu.SemaphoreType.DMA((NWIN,)),
            pltpu.SemaphoreType.DMA((NWIN,)),
        ],
        compiler_params=pltpu.CompilerParams(vmem_limit_bytes=60 * 2**20),
        name="cut_first",
    )(key, value)


def gate_kernel(*refs):
    del refs


def gate(passed, *waited):
    return pl.pallas_call(
        gate_kernel,
        in_specs=[ANY] * (1 + len(waited)),
        out_specs=ANY,
        out_shape=jax.ShapeDtypeStruct(passed.shape, passed.dtype),
        input_output_aliases={0: 0},
        compiler_params=SMALL,
        name="gate",
    )(passed, *waited)


def cut_kernel(whole_ref, piece_ref, out_ref):
    heads = out_ref.shape[1] - piece_ref.shape[1]
    for window in range(NWIN):
        rows = pl.ds(window * POSITIONS, POSITIONS)
        for part in range(SPAN):
            for head in range(heads):
                lanes = pl.ds((part * PARTS + head) * HD, HD)
                out_ref[window * SPAN + part, head] = whole_ref[rows, lanes]
    out_ref[:, heads:] = piece_ref[...]


def cut(whole, piece, flops):
    slabs = PARTS + piece.shape[1]
    return pl.pallas_call(
        cut_kernel,
        in_specs=[VMEM] * 2,
        out_specs=VMEM,
        out_shape=jax.ShapeDtypeStruct((NWIN * SPAN, slabs, POSITIONS, HD), jnp.bfloat16),
        compiler_params=PARAMS,
        cost_estimate=pl.CostEstimate(flops=flops, bytes_accessed=2**21, transcendentals=0),
        name="cut",
    )(whole, piece)


def paste_kernel(in_ref, out_ref, held_ref, sems):
    copies = []
    for window in range(NWIN):
        rows = pl.ds(window * POSITIONS, POSITIONS)
        for part in range(SPAN):
            for head in range(PARTS):
                lanes = pl.ds((part * PARTS + head) * HD, HD)
                held_ref[rows, lanes] = in_ref[window * SPAN + part, head]
        copies.append(
            pltpu.make_async_copy(held_ref.at[rows], out_ref.at[rows], sems.at[window])
        )
        copies[-1].start()
    for copy in copies:
        copy.wait()


def paste(pieces):
    return pl.pallas_call(
        paste_kernel,
        in_specs=[VMEM],
        out_specs=ANY,
        out_shape=jax.ShapeDtypeStruct((POS, HEADS * HD), jnp.bfloat16),
        scratch_shapes=[
            pltpu.VMEM((POS, HEADS * HD), jnp.bfloat16),
            pltpu.SemaphoreType.DMA((NWIN,)),
        ],
        compiler_params=PARAMS,
        name="paste",
    )(pieces)


def body(query_vectors, key_vectors, value_vectors, chosen_groups, chosen_count):
    group_devices = lax.axis_size("grp")

    def to_peers(block):
        return lax.all_to_all(block, "ctx", split_axis=0, concat_axis=0, tiled=True)

    def up(block):
        return lax.ppermute(block, "grp", [(at, at + 1) for at in range(group_devices - 1)])

    def down(block):
        return lax.ppermute(block, "grp", [(at + 1, at) for at in range(group_devices - 1)])

    later_query = down(query_vectors)
    first, last = cut_first(key_vectors, value_vectors)
    last_up = up(last)
    first = to_peers(first)
    first_up = up(first)
    flags = make_flags(chosen_groups, chosen_count)
    second = to_peers(gate(cut(later_query, last_up, 10**11), first, flags))
    third = to_peers(gate(cut(query_vectors, last, 10**6), second))
    ahead_b = attend_ahead(flags, 1, second, 2, second, 3)
    far_b = up(ahead_b)
    far_a = up(attend_ahead(flags, 2, second, 0, first_up, 0, ahead_b))
    near_b, log_b = attend_near(flags, 1, third, 2, third, 3, second, 3)
    near_a, log_a = attend_near(flags, 2, third, 0, first, 0, first_up, 0)
    merged = merge(flags, (near_a, near_b), (log_a, log_b), (far_a, far_b))
    return paste(to_peers(merged))


def solution(mesh):
    in_specs = (P(("grp", "ctx"), None), P(("grp", "ctx"), None), P(("grp", "ctx"), None), P(), P())
    out_specs = P(("grp", "ctx"), None)
    return jax.shard_map(body, mesh=mesh, in_specs=in_specs, out_specs=out_specs, check_vma=False)
```

```python
import functools
import math

import jax
import jax.numpy as jnp
from jax import lax
from jax.experimental import pallas as pl
from jax.experimental.pallas import tpu as pltpu
from jax.sharding import PartitionSpec as P

HEADS = 12
HD = 128
POS = 256
SPAN = 4
NWIN = 8
LOOK = 2
QB = 256
PARTS = HEADS // SPAN
POSITIONS = POS // NWIN
STAT_ROWS = 32
LOG2E = math.log2(math.e)
FACTOR = HD**-0.5 * LOG2E
NEG_FILL = -1e30
SMEM = pl.BlockSpec(memory_space=pltpu.SMEM)
VMEM = pl.BlockSpec(memory_space=pltpu.VMEM)
ANY = pl.BlockSpec(memory_space=pl.ANY)
HBM = pl.BlockSpec(memory_space=pltpu.HBM)
SMALL = pltpu.CompilerParams(vmem_limit_bytes=2**20)
PARAMS = pltpu.CompilerParams(vmem_limit_bytes=14 * 2**20)


def is_taken(groups_ref, count_ref, group, distance):
    groups = groups_ref.shape[0]
    window = lax.axis_index("ctx") // SPAN
    held = jnp.minimum(group, groups - 1)
    source = group - distance
    count = count_ref[held, window]
    taken = jnp.bool_(False)
    for slot in range(LOOK):
        taken = taken | ((groups_ref[held, window, slot] == source) & (slot < count))
    return taken & (source >= 0) & (group < groups)


def flags_kernel(groups_ref, count_ref, out_ref):
    group = lax.axis_index("grp")
    for at, (owner, distance) in enumerate(((group, 1), (group, 2), (group + 1, 2))):
        out_ref[at] = is_taken(groups_ref, count_ref, owner, distance).astype(jnp.int32)
    out_ref[3] = jnp.int32(0)


def make_flags(groups, count):
    return pl.pallas_call(
        flags_kernel,
        in_specs=[SMEM] * 2,
        out_specs=SMEM,
        out_shape=jax.ShapeDtypeStruct((4,), jnp.int32),
        compiler_params=SMALL,
        name="flags",
    )(groups, count)


def score(query, keys):
    return lax.dot_general(
        keys, query, (((1,), (1,)), ((), ())), preferred_element_type=jnp.float32
    )


def soften(score_ref, values, diagonal=False):
    count = values.shape[0]
    scores = score_ref[:count, :]
    if diagonal:
        tail = scores[count - QB :]
        frame_key = lax.broadcasted_iota(jnp.int32, (QB, QB), 0) // POSITIONS
        frame_query = lax.broadcasted_iota(jnp.int32, (QB, QB), 1) // POSITIONS
        tail = jnp.where(frame_query >= frame_key, tail, NEG_FILL)
        scores = jnp.concatenate([scores[: count - QB], tail], axis=0) if count > QB else tail
    highest = jnp.max(scores, axis=0, keepdims=True)
    weights = jnp.exp2((scores - highest) * FACTOR)
    summed = jnp.sum(weights, axis=0, keepdims=True)
    blended = lax.dot_general(
        values,
        weights.astype(jnp.bfloat16),
        (((0,), (0,)), ((), ())),
        preferred_element_type=jnp.float32,
    )
    return highest, summed, blended


def in_turn(jobs, score_refs, done):
    def begin(at):
        scores = jobs[at][0]()
        score_refs[at % 2][: scores.shape[0], :] = scores

    begin(0)
    for at, (_, finish) in enumerate(jobs):
        if at + 1 < len(jobs):
            begin(at + 1)
        done(at, finish(score_refs[at % 2]))


def buffers(rows):
    return [pltpu.VMEM((rows, QB), jnp.float32)] * 2


def join(old, new):
    ceiling = jnp.maximum(old[0], new[0])
    old_scale = jnp.exp2((old[0] - ceiling) * FACTOR)
    new_scale = jnp.exp2((new[0] - ceiling) * FACTOR)
    return (
        ceiling,
        old[1] * old_scale + new[1] * new_scale,
        old[2] * old_scale + new[2] * new_scale,
    )


def put_blocks(ref, head, start, value):
    for at in range(0, QB, HD):
        ref[head, pl.ds(start + at, HD), :] = value[:, at : at + HD].astype(ref.dtype)


def rows_of(ref, slab, start, size):
    first, count = start // POSITIONS, size // POSITIONS
    return ref[pl.ds(first, count), slab].reshape(size, HD)


def log_rows(part):
    log_sum = part[0] * FACTOR + jnp.log(part[1]) * LOG2E
    return [log_sum[:, at : at + HD] for at in range(0, QB, HD)]


def ahead_kernel(query_slab, pair_slab, flags_ref, q_ref, kv_ref, *rest):
    out_ref, score_refs = rest[-3], rest[-2:]
    rows = q_ref.shape[0] * POSITIONS
    heads = out_ref.shape[0]
    taken = flags_ref[2] > 0

    @pl.when(taken)
    def _():
        @pl.loop(0, heads)
        def _(head):
            keys = kv_ref[:, pair_slab + 2 * head].reshape(rows, HD)
            values = kv_ref[:, pair_slab + 2 * head + 1].reshape(rows, HD)

            def job(start):
                return (
                    lambda: score(rows_of(q_ref, query_slab + head, start, QB), keys),
                    lambda scores: soften(scores, values),
                )

            logs = []

            def done(at, part):
                put_blocks(out_ref, head, at * QB, part[2] / part[1])
                logs.extend(log_rows(part))

            in_turn([job(start) for start in range(0, rows, QB)], score_refs, done)
            left = jnp.concatenate(logs, axis=0)
            pieces = []
            for _ in range(3):
                pieces.append(left.astype(jnp.bfloat16).astype(jnp.float32))
                left = left - pieces[-1]
            pieces.append(jnp.zeros((STAT_ROWS - 3 * left.shape[0], HD), jnp.float32))
            packed = jnp.concatenate(pieces, axis=0).astype(jnp.bfloat16)
            out_ref[head, pl.ds(rows, STAT_ROWS), :] = packed

    @pl.when(jnp.logical_not(taken))
    def _():
        out_ref[:, pl.ds(rows, STAT_ROWS), :] = jnp.zeros((heads, STAT_ROWS, HD), jnp.bfloat16)


def near_kernel(query_slab, own_slab, up_slab, flags_ref, q_ref, own_ref, up_ref, out_ref, log_ref, *score_refs):
    rows = q_ref.shape[0] * POSITIONS
    heads = out_ref.shape[0]
    taken = flags_ref[0] > 0

    def run(with_earlier):
        @pl.loop(0, heads)
        def _(head):
            def own(start):
                def begin():
                    query = rows_of(q_ref, query_slab + head, start, QB)
                    return score(query, rows_of(own_ref, own_slab + 2 * head, 0, start + QB))

                def finish(scores):
                    return soften(scores, rows_of(own_ref, own_slab + 2 * head + 1, 0, start + QB), True)

                return begin, finish

            def earlier(start):
                def begin():
                    query = rows_of(q_ref, query_slab + head, start, QB)
                    return score(query, rows_of(up_ref, up_slab + 2 * head, 0, rows))

                def finish(scores):
                    return soften(scores, rows_of(up_ref, up_slab + 2 * head + 1, 0, rows))

                return begin, finish

            logs = []
            held = []

            def done(at, part):
                if with_earlier:
                    held.append(part)
                    if at % 2 == 0:
                        return
                    part = join(held[-2], held[-1])
                    at = at // 2
                put_blocks(out_ref, head, at * QB, part[2] / part[1])
                logs.extend(log_rows(part))

            jobs = []
            for start in range(0, rows, QB):
                jobs.append(own(start))
                if with_earlier:
                    jobs.append(earlier(start))
            in_turn(jobs, score_refs, done)
            log_ref[head] = jnp.concatenate(logs, axis=0)

    @pl.when(taken)
    def _():
        run(True)

    @pl.when(jnp.logical_not(taken))
    def _():
        run(False)


def merge_kernel(flags_ref, near_a, near_b, log_a, log_b, far_a, far_b, out_ref):
    rows = near_a.shape[1]
    blocks = rows // HD
    taken = flags_ref[1] > 0

    def put(head, block, value):
        count = HD // POSITIONS
        frames = pl.ds(block * count, count)
        turned = jnp.transpose(value).astype(jnp.bfloat16)
        out_ref[frames, head] = turned.reshape(count, POSITIONS, HD)

    def each_head():
        count = near_a.shape[0]
        for head in range(PARTS):
            refs = (near_a, log_a, far_a) if head < count else (near_b, log_b, far_b)
            yield (head,) + tuple(ref.at[head if head < count else head - count] for ref in refs)

    @pl.when(taken)
    def _():
        for head, near_ref, log_ref, far_ref in each_head():
            pieces = far_ref[pl.ds(rows, STAT_ROWS), :].astype(jnp.float32)
            far_log = pieces[:blocks] + pieces[blocks : 2 * blocks] + pieces[2 * blocks : 3 * blocks]
            shares = 1.0 / (1.0 + jnp.exp2(log_ref[...] - far_log))
            for block in range(blocks):
                part = pl.ds(block * HD, HD)
                near = near_ref[part, :]
                far = far_ref[part, :].astype(jnp.float32)
                put(head, block, near + (far - near) * shares[block : block + 1])

    @pl.when(jnp.logical_not(taken))
    def _():
        for head, near_ref, _, _ in each_head():
            for block in range(blocks):
                put(head, block, near_ref[pl.ds(block * HD, HD), :])


def cost(passes, rows, heads, moved):
    return pl.CostEstimate(
        flops=int(4 * passes * rows * rows * heads * HD),
        bytes_accessed=moved,
        transcendentals=int(passes * rows * rows * heads),
    )


def attend_ahead(flags, heads, query, query_slab, pair, pair_slab, *waited):
    rows = pair.shape[0] * POSITIONS
    return pl.pallas_call(
        functools.partial(ahead_kernel, query_slab, pair_slab),
        in_specs=[SMEM] + [VMEM] * 2 + [ANY] * len(waited),
        out_specs=VMEM,
        out_shape=jax.ShapeDtypeStruct((heads, rows + STAT_ROWS, HD), jnp.bfloat16),
        scratch_shapes=buffers(rows),
        compiler_params=PARAMS,
        cost_estimate=cost(1, rows, heads, rows * heads * HD * 8),
        name="ahead",
    )(flags, query, pair, *waited)


def attend_near(flags, heads, query, query_slab, own, own_slab, up, up_slab):
    rows = query.shape[0] * POSITIONS
    return pl.pallas_call(
        functools.partial(near_kernel, query_slab, own_slab, up_slab),
        in_specs=[SMEM] + [VMEM] * 3,
        out_specs=[VMEM] * 2,
        out_shape=[
            jax.ShapeDtypeStruct((heads, rows, HD), jnp.float32),
            jax.ShapeDtypeStruct((heads, rows // HD, HD), jnp.float32),
        ],
        scratch_shapes=buffers(rows),
        compiler_params=PARAMS,
        cost_estimate=cost(1.6, rows, heads, rows * heads * HD * 14),
        name="near",
    )(flags, query, own, up)


def merge(flags, near, logs, far):
    rows = near[0].shape[1]
    return pl.pallas_call(
        merge_kernel,
        in_specs=[SMEM] + [VMEM] * 6,
        out_specs=VMEM,
        out_shape=jax.ShapeDtypeStruct((rows // POSITIONS, PARTS, POSITIONS, HD), jnp.bfloat16),
        compiler_params=PARAMS,
        cost_estimate=cost(0, rows, PARTS, rows * PARTS * HD * 8),
        name="merge",
    )(flags, *near, *logs, *far)


def cut_first_kernel(k_ref, v_ref, first_ref, last_ref, held_ref, first_piece, last_piece, *sems):
    in_sems, first_sems, last_sems = sems

    def fetch(which, window):
        rows = pl.ds(window * POSITIONS, POSITIONS)
        ref = (k_ref, v_ref)[which]
        return pltpu.make_async_copy(
            ref.at[rows], held_ref.at[which, rows], in_sems.at[which, window]
        )

    def stores(window):
        peers = pl.ds(window * SPAN, SPAN)
        return (
            pltpu.make_async_copy(first_piece.at[peers], first_ref.at[peers], first_sems.at[window]),
            pltpu.make_async_copy(last_piece.at[peers], last_ref.at[peers], last_sems.at[window]),
        )

    for window in range(NWIN):
        for which in range(2):
            fetch(which, window).start()
    for window in range(NWIN):
        rows = pl.ds(window * POSITIONS, POSITIONS)
        for which in range(2):
            fetch(which, window).wait()
            for part in range(SPAN):
                for head in range(PARTS):
                    lanes = pl.ds((part * PARTS + head) * HD, HD)
                    value = held_ref[which, rows, lanes]
                    if head < 2:
                        first_piece[window * SPAN + part, 2 * head + which] = value
                    else:
                        last_piece[window * SPAN + part, which] = value
        for copy in stores(window):
            copy.start()
    for window in range(NWIN):
        for copy in stores(window):
            copy.wait()


def cut_first(key, value):
    first = (NWIN * SPAN, 4, POSITIONS, HD)
    last = (NWIN * SPAN, 2, POSITIONS, HD)
    return pl.pallas_call(
        cut_first_kernel,
        in_specs=[HBM] * 2,
        out_specs=[HBM] * 2,
        out_shape=[jax.ShapeDtypeStruct(shape, jnp.bfloat16) for shape in (first, last)],
        scratch_shapes=[
            pltpu.VMEM((2,) + key.shape, jnp.bfloat16),
            pltpu.VMEM(first, jnp.bfloat16),
            pltpu.VMEM(last, jnp.bfloat16),
            pltpu.SemaphoreType.DMA((2, NWIN)),
            pltpu.SemaphoreType.DMA((NWIN,)),
            pltpu.SemaphoreType.DMA((NWIN,)),
        ],
        compiler_params=pltpu.CompilerParams(vmem_limit_bytes=60 * 2**20),
        name="cut_first",
    )(key, value)


def gate_kernel(*refs):
    del refs


def gate(passed, *waited):
    return pl.pallas_call(
        gate_kernel,
        in_specs=[ANY] * (1 + len(waited)),
        out_specs=ANY,
        out_shape=jax.ShapeDtypeStruct(passed.shape, passed.dtype),
        input_output_aliases={0: 0},
        compiler_params=SMALL,
        name="gate",
    )(passed, *waited)


def cut_kernel(whole_ref, piece_ref, out_ref):
    heads = out_ref.shape[1] - piece_ref.shape[1]
    for window in range(NWIN):
        rows = pl.ds(window * POSITIONS, POSITIONS)
        for part in range(SPAN):
            for head in range(heads):
                lanes = pl.ds((part * PARTS + head) * HD, HD)
                out_ref[window * SPAN + part, head] = whole_ref[rows, lanes]
    out_ref[:, heads:] = piece_ref[...]


def cut(whole, piece, flops):
    slabs = PARTS + piece.shape[1]
    return pl.pallas_call(
        cut_kernel,
        in_specs=[VMEM] * 2,
        out_specs=VMEM,
        out_shape=jax.ShapeDtypeStruct((NWIN * SPAN, slabs, POSITIONS, HD), jnp.bfloat16),
        compiler_params=PARAMS,
        cost_estimate=pl.CostEstimate(flops=flops, bytes_accessed=2**21, transcendentals=0),
        name="cut",
    )(whole, piece)


def paste_kernel(in_ref, out_ref, held_ref, sems):
    copies = []
    for window in range(NWIN):
        rows = pl.ds(window * POSITIONS, POSITIONS)
        for part in range(SPAN):
            for head in range(PARTS):
                lanes = pl.ds((part * PARTS + head) * HD, HD)
                held_ref[rows, lanes] = in_ref[window * SPAN + part, head]
        copies.append(
            pltpu.make_async_copy(held_ref.at[rows], out_ref.at[rows], sems.at[window])
        )
        copies[-1].start()
    for copy in copies:
        copy.wait()


def paste(pieces):
    return pl.pallas_call(
        paste_kernel,
        in_specs=[VMEM],
        out_specs=ANY,
        out_shape=jax.ShapeDtypeStruct((POS, HEADS * HD), jnp.bfloat16),
        scratch_shapes=[
            pltpu.VMEM((POS, HEADS * HD), jnp.bfloat16),
            pltpu.SemaphoreType.DMA((NWIN,)),
        ],
        compiler_params=PARAMS,
        name="paste",
    )(pieces)


def body(query_vectors, key_vectors, value_vectors, chosen_groups, chosen_count):
    group_devices = lax.axis_size("grp")

    def to_peers(block):
        return lax.all_to_all(block, "ctx", split_axis=0, concat_axis=0, tiled=True)

    def up(block):
        return lax.ppermute(block, "grp", [(at, at + 1) for at in range(group_devices - 1)])

    def down(block):
        return lax.ppermute(block, "grp", [(at + 1, at) for at in range(group_devices - 1)])

    later_query = down(query_vectors)
    first, last = cut_first(key_vectors, value_vectors)
    last_up = up(last)
    first = to_peers(first)
    first_up = up(first)
    flags = make_flags(chosen_groups, chosen_count)
    second = to_peers(gate(cut(later_query, last_up, 10**11), first, flags))
    third = to_peers(gate(cut(query_vectors, last, 10**6), second))
    ahead_b = attend_ahead(flags, 1, second, 2, second, 3)
    far_b = up(ahead_b)
    far_a = up(attend_ahead(flags, 2, second, 0, first_up, 0, ahead_b))
    near_b, log_b = attend_near(flags, 1, third, 2, third, 3, second, 3)
    near_a, log_a = attend_near(flags, 2, third, 0, first, 0, first_up, 0)
    merged = merge(flags, (near_a, near_b), (log_a, log_b), (far_a, far_b))
    return paste(to_peers(merged))


def solution(mesh):
    in_specs = (P(("grp", "ctx"), None), P(("grp", "ctx"), None), P(("grp", "ctx"), None), P(), P())
    out_specs = P(("grp", "ctx"), None)
    return jax.shard_map(body, mesh=mesh, in_specs=in_specs, out_specs=out_specs, check_vma=False)
```

```python
import functools
import math

import jax
import jax.numpy as jnp
from jax import lax
from jax.experimental import pallas as pl
from jax.experimental.pallas import tpu as pltpu
from jax.sharding import PartitionSpec as P

HEADS = 12
HD = 128
POS = 256
SPAN = 4
NWIN = 8
LOOK = 2
QB = 256
PARTS = HEADS // SPAN
POSITIONS = POS // NWIN
STAT_ROWS = 32
LOG2E = math.log2(math.e)
FACTOR = HD**-0.5 * LOG2E
NEG_FILL = -1e30
SMEM = pl.BlockSpec(memory_space=pltpu.SMEM)
VMEM = pl.BlockSpec(memory_space=pltpu.VMEM)
ANY = pl.BlockSpec(memory_space=pl.ANY)
HBM = pl.BlockSpec(memory_space=pltpu.HBM)
SMALL = pltpu.CompilerParams(vmem_limit_bytes=2**20)
PARAMS = pltpu.CompilerParams(vmem_limit_bytes=10 * 2**20)


def is_taken(groups_ref, count_ref, group, distance):
    groups = groups_ref.shape[0]
    window = lax.axis_index("ctx") // SPAN
    held = jnp.minimum(group, groups - 1)
    source = group - distance
    count = count_ref[held, window]
    taken = jnp.bool_(False)
    for slot in range(LOOK):
        taken = taken | ((groups_ref[held, window, slot] == source) & (slot < count))
    return taken & (source >= 0) & (group < groups)


def flags_kernel(groups_ref, count_ref, out_ref):
    group = lax.axis_index("grp")
    for at, (owner, distance) in enumerate(((group, 1), (group, 2), (group + 1, 2))):
        out_ref[at] = is_taken(groups_ref, count_ref, owner, distance).astype(jnp.int32)
    out_ref[3] = jnp.int32(0)


def make_flags(groups, count):
    return pl.pallas_call(
        flags_kernel,
        in_specs=[SMEM] * 2,
        out_specs=SMEM,
        out_shape=jax.ShapeDtypeStruct((4,), jnp.int32),
        compiler_params=SMALL,
        name="flags",
    )(groups, count)


def score(query, keys):
    return lax.dot_general(
        query, keys, (((1,), (1,)), ((), ())), preferred_element_type=jnp.float32
    )


def soften(scores, values, diagonal=False):
    if diagonal:
        rows, count = scores.shape
        tail = scores[:, count - rows :]
        frame_query = lax.broadcasted_iota(jnp.int32, (rows, rows), 0) // POSITIONS
        frame_key = lax.broadcasted_iota(jnp.int32, (rows, rows), 1) // POSITIONS
        tail = jnp.where(frame_query >= frame_key, tail, NEG_FILL)
        scores = jnp.concatenate([scores[:, : count - rows], tail], axis=1) if count > rows else tail
    highest = jnp.max(scores, axis=-1, keepdims=True)
    weights = jnp.exp2((scores - highest) * FACTOR)
    beside = jnp.concatenate([values, jnp.ones_like(values)], axis=1)
    product = jnp.dot(weights.astype(jnp.bfloat16), beside, preferred_element_type=jnp.float32)
    return highest, product[:, HD:], product[:, :HD]


def in_turn(jobs, done):
    scores = jobs[0][0]()
    for at, (_, finish) in enumerate(jobs):
        following = jobs[at + 1][0]() if at + 1 < len(jobs) else None
        done(at, finish(scores))
        scores = following


def join(old, new):
    ceiling = jnp.maximum(old[0], new[0])
    old_scale = jnp.exp2((old[0] - ceiling) * FACTOR)
    new_scale = jnp.exp2((new[0] - ceiling) * FACTOR)
    return (
        ceiling,
        old[1] * old_scale + new[1] * new_scale,
        old[2] * old_scale + new[2] * new_scale,
    )


def rows_of(ref, slab, start, size):
    first, count = start // POSITIONS, size // POSITIONS
    return ref[pl.ds(first, count), slab].reshape(size, HD)


def eye_mask():
    return lax.broadcasted_iota(jnp.int32, (HD, HD), 0) == lax.broadcasted_iota(
        jnp.int32, (HD, HD), 1
    )


def log_rows(part):
    log_sum = part[0] * FACTOR + jnp.log(part[1]) * LOG2E
    return [
        jnp.sum(jnp.where(eye_mask(), log_sum[at : at + HD], 0.0), axis=0, keepdims=True)
        for at in range(0, log_sum.shape[0], HD)
    ]


def ahead_kernel(query_slab, pair_slab, flags_ref, q_ref, kv_ref, *rest):
    out_ref = rest[-1]
    rows = q_ref.shape[0] * POSITIONS
    heads = out_ref.shape[0]
    taken = flags_ref[2] > 0

    @pl.when(taken)
    def _():
        @pl.loop(0, heads)
        def _(head):
            keys = kv_ref[:, pair_slab + 2 * head].reshape(rows, HD)
            values = kv_ref[:, pair_slab + 2 * head + 1].reshape(rows, HD)

            def job(start):
                return (
                    lambda: score(rows_of(q_ref, query_slab + head, start, QB), keys),
                    lambda scores: soften(scores, values),
                )

            logs = []

            def done(at, part):
                out_ref[head, pl.ds(at * QB, QB), :] = (part[2] / part[1]).astype(jnp.bfloat16)
                logs.extend(log_rows(part))

            in_turn([job(start) for start in range(0, rows, QB)], done)
            left = jnp.concatenate(logs, axis=0)
            pieces = []
            for _ in range(3):
                pieces.append(left.astype(jnp.bfloat16).astype(jnp.float32))
                left = left - pieces[-1]
            pieces.append(jnp.zeros((STAT_ROWS - 3 * left.shape[0], HD), jnp.float32))
            packed = jnp.concatenate(pieces, axis=0).astype(jnp.bfloat16)
            out_ref[head, pl.ds(rows, STAT_ROWS), :] = packed

    @pl.when(jnp.logical_not(taken))
    def _():
        out_ref[:, pl.ds(rows, STAT_ROWS), :] = jnp.zeros((heads, STAT_ROWS, HD), jnp.bfloat16)


def near_kernel(query_slab, own_slab, up_slab, flags_ref, q_ref, own_ref, up_ref, out_ref, log_ref):
    rows = q_ref.shape[0] * POSITIONS
    heads = out_ref.shape[0]
    taken = flags_ref[0] > 0

    def run(with_earlier):
        @pl.loop(0, heads)
        def _(head):
            def own(start):
                def begin():
                    query = rows_of(q_ref, query_slab + head, start, QB)
                    return score(query, rows_of(own_ref, own_slab + 2 * head, 0, start + QB))

                def finish(scores):
                    return soften(scores, rows_of(own_ref, own_slab + 2 * head + 1, 0, start + QB), True)

                return begin, finish

            def earlier(start):
                def begin():
                    query = rows_of(q_ref, query_slab + head, start, QB)
                    return score(query, rows_of(up_ref, up_slab + 2 * head, 0, rows))

                def finish(scores):
                    return soften(scores, rows_of(up_ref, up_slab + 2 * head + 1, 0, rows))

                return begin, finish

            logs = []
            held = []

            def done(at, part):
                if with_earlier:
                    held.append(part)
                    if at % 2 == 0:
                        return
                    part = join(held[-2], held[-1])
                    at = at // 2
                out_ref[head, pl.ds(at * QB, QB), :] = part[2] / part[1]
                logs.extend(log_rows(part))

            jobs = []
            for start in range(0, rows, QB):
                jobs.append(own(start))
                if with_earlier:
                    jobs.append(earlier(start))
            in_turn(jobs, done)
            log_ref[head] = jnp.concatenate(logs, axis=0)

    @pl.when(taken)
    def _():
        run(True)

    @pl.when(jnp.logical_not(taken))
    def _():
        run(False)


def merge_kernel(flags_ref, near_ref, log_ref, far_ref, *rest):
    out_ref = rest[-1]
    heads, rows, _ = near_ref.shape
    blocks = rows // HD
    taken = flags_ref[1] > 0

    def put(head, block, value):
        count = HD // POSITIONS
        frames = pl.ds(block * count, count)
        out_ref[frames, head] = value.astype(jnp.bfloat16).reshape(count, POSITIONS, HD)

    for other in rest[:-1]:
        out_ref[:, heads:] = other[...]

    @pl.when(taken)
    def _():
        for head in range(heads):
            pieces = far_ref[head, pl.ds(rows, STAT_ROWS), :].astype(jnp.float32)
            far_log = pieces[:blocks] + pieces[blocks : 2 * blocks] + pieces[2 * blocks : 3 * blocks]
            shares = jnp.transpose(1.0 / (1.0 + jnp.exp2(log_ref[head] - far_log)))
            for block in range(blocks):
                part = pl.ds(block * HD, HD)
                near = near_ref[head, part, :]
                far = far_ref[head, part, :].astype(jnp.float32)
                put(head, block, near + (far - near) * shares[:, block : block + 1])

    @pl.when(jnp.logical_not(taken))
    def _():
        for head in range(heads):
            for block in range(blocks):
                put(head, block, near_ref[head, pl.ds(block * HD, HD), :])


def near_merged_kernel(query_slab, own_slab, up_slab, flags_ref, q_ref, own_ref, up_ref, *rest):
    far_ref, out_ref, near_ref, log_ref = rest
    near_kernel(
        query_slab, own_slab, up_slab, flags_ref, q_ref, own_ref, up_ref, near_ref, log_ref
    )
    merge_kernel(flags_ref, near_ref, log_ref, far_ref, out_ref)


def cost(passes, rows, heads, moved):
    return pl.CostEstimate(
        flops=int(4 * passes * rows * rows * heads * HD),
        bytes_accessed=moved,
        transcendentals=int(passes * rows * rows * heads),
    )


def attend_ahead(flags, heads, passes, query, query_slab, pair, pair_slab, *waited):
    rows = pair.shape[0] * POSITIONS
    return pl.pallas_call(
        functools.partial(ahead_kernel, query_slab, pair_slab),
        in_specs=[SMEM] + [VMEM] * 2 + [ANY] * len(waited),
        out_specs=VMEM,
        out_shape=jax.ShapeDtypeStruct((heads, rows + STAT_ROWS, HD), jnp.bfloat16),
        compiler_params=PARAMS,
        cost_estimate=cost(passes, rows, heads, rows * heads * HD * 8),
        name="ahead",
    )(flags, query, pair, *waited)


def attend_near(flags, heads, query, query_slab, own, own_slab, up, up_slab):
    rows = query.shape[0] * POSITIONS
    return pl.pallas_call(
        functools.partial(near_kernel, query_slab, own_slab, up_slab),
        in_specs=[SMEM] + [VMEM] * 3,
        out_specs=[VMEM] * 2,
        out_shape=[
            jax.ShapeDtypeStruct((heads, rows, HD), jnp.float32),
            jax.ShapeDtypeStruct((heads, rows // HD, HD), jnp.float32),
        ],
        compiler_params=PARAMS,
        cost_estimate=cost(160, rows, heads, rows * heads * HD * 14),
        name="near",
    )(flags, query, own, up)


def attend_near_merged(flags, query, query_slab, own, own_slab, up, up_slab, far):
    frames = query.shape[0]
    rows = frames * POSITIONS
    return pl.pallas_call(
        functools.partial(near_merged_kernel, query_slab, own_slab, up_slab),
        in_specs=[SMEM] + [VMEM] * 4,
        out_specs=VMEM,
        out_shape=jax.ShapeDtypeStruct((frames, 1, POSITIONS, HD), jnp.bfloat16),
        scratch_shapes=[
            pltpu.VMEM((1, rows, HD), jnp.float32),
            pltpu.VMEM((1, rows // HD, HD), jnp.float32),
        ],
        compiler_params=PARAMS,
        cost_estimate=cost(1.6, rows, 1, rows * HD * 14),
        name="near_merged",
    )(flags, query, own, up, far)


def merge(flags, near, logs, far, *others):
    heads, rows, _ = near.shape
    slabs = heads + sum(other.shape[1] for other in others)
    return pl.pallas_call(
        merge_kernel,
        in_specs=[SMEM] + [VMEM] * (3 + len(others)),
        out_specs=VMEM,
        out_shape=jax.ShapeDtypeStruct((rows // POSITIONS, slabs, POSITIONS, HD), jnp.bfloat16),
        compiler_params=PARAMS,
        cost_estimate=cost(0, rows, heads, rows * heads * HD * 8),
        name="merge",
    )(flags, near, logs, far, *others)


def cut_first_kernel(k_ref, v_ref, first_ref, last_ref, held_ref, first_piece, last_piece, *sems):
    in_sems, first_sems, last_sems = sems

    def fetch(which, window):
        rows = pl.ds(window * POSITIONS, POSITIONS)
        ref = (k_ref, v_ref)[which]
        return pltpu.make_async_copy(
            ref.at[rows], held_ref.at[which, rows], in_sems.at[which, window]
        )

    def stores(window):
        peers = pl.ds(window * SPAN, SPAN)
        return (
            pltpu.make_async_copy(first_piece.at[peers], first_ref.at[peers], first_sems.at[window]),
            pltpu.make_async_copy(last_piece.at[peers], last_ref.at[peers], last_sems.at[window]),
        )

    for window in range(NWIN):
        for which in range(2):
            fetch(which, window).start()
    for window in range(NWIN):
        rows = pl.ds(window * POSITIONS, POSITIONS)
        for which in range(2):
            fetch(which, window).wait()
            for part in range(SPAN):
                for head in range(PARTS):
                    lanes = pl.ds((part * PARTS + head) * HD, HD)
                    value = held_ref[which, rows, lanes]
                    if head < 2:
                        first_piece[window * SPAN + part, 2 * head + which] = value
                    else:
                        last_piece[window * SPAN + part, which] = value
        for copy in stores(window):
            copy.start()
    for window in range(NWIN):
        for copy in stores(window):
            copy.wait()


def cut_first(key, value):
    first = (NWIN * SPAN, 4, POSITIONS, HD)
    last = (NWIN * SPAN, 2, POSITIONS, HD)
    return pl.pallas_call(
        cut_first_kernel,
        in_specs=[HBM] * 2,
        out_specs=[HBM] * 2,
        out_shape=[jax.ShapeDtypeStruct(shape, jnp.bfloat16) for shape in (first, last)],
        scratch_shapes=[
            pltpu.VMEM((2,) + key.shape, jnp.bfloat16),
            pltpu.VMEM(first, jnp.bfloat16),
            pltpu.VMEM(last, jnp.bfloat16),
            pltpu.SemaphoreType.DMA((2, NWIN)),
            pltpu.SemaphoreType.DMA((NWIN,)),
            pltpu.SemaphoreType.DMA((NWIN,)),
        ],
        compiler_params=pltpu.CompilerParams(vmem_limit_bytes=60 * 2**20),
        name="cut_first",
    )(key, value)


def gate_kernel(*refs):
    del refs


def gate(space, passed, *waited):
    return pl.pallas_call(
        gate_kernel,
        in_specs=[space] + [ANY] * len(waited),
        out_specs=space,
        out_shape=jax.ShapeDtypeStruct(passed.shape, passed.dtype),
        input_output_aliases={0: 0},
        compiler_params=SMALL,
        name="gate",
    )(passed, *waited)


def cut_kernel(whole_ref, piece_ref, out_ref):
    heads = out_ref.shape[1] - piece_ref.shape[1]
    for window in range(NWIN):
        rows = pl.ds(window * POSITIONS, POSITIONS)
        for part in range(SPAN):
            for head in range(heads):
                lanes = pl.ds((part * PARTS + head) * HD, HD)
                out_ref[window * SPAN + part, head] = whole_ref[rows, lanes]
    out_ref[:, heads:] = piece_ref[...]


def cut(whole, piece, flops):
    slabs = PARTS + piece.shape[1]
    return pl.pallas_call(
        cut_kernel,
        in_specs=[VMEM] * 2,
        out_specs=VMEM,
        out_shape=jax.ShapeDtypeStruct((NWIN * SPAN, slabs, POSITIONS, HD), jnp.bfloat16),
        compiler_params=PARAMS,
        cost_estimate=pl.CostEstimate(flops=flops, bytes_accessed=2**21, transcendentals=0),
        name="cut",
    )(whole, piece)


def cut_out_kernel(whole_ref, piece_ref, out_ref, held_ref, sem):
    cut_kernel(whole_ref, piece_ref, held_ref)
    copy = pltpu.make_async_copy(held_ref, out_ref, sem)
    copy.start()
    copy.wait()


def cut_out(whole, piece):
    shape = (NWIN * SPAN, PARTS + piece.shape[1], POSITIONS, HD)
    return pl.pallas_call(
        cut_out_kernel,
        in_specs=[VMEM] * 2,
        out_specs=HBM,
        out_shape=jax.ShapeDtypeStruct(shape, jnp.bfloat16),
        scratch_shapes=[pltpu.VMEM(shape, jnp.bfloat16), pltpu.SemaphoreType.DMA],
        compiler_params=pltpu.CompilerParams(vmem_limit_bytes=60 * 2**20),
        cost_estimate=pl.CostEstimate(flops=10**6, bytes_accessed=2**21, transcendentals=0),
        name="cut_out",
    )(whole, piece)


def paste_kernel(in_ref, out_ref, held_ref, sems):
    copies = []
    for window in range(NWIN):
        rows = pl.ds(window * POSITIONS, POSITIONS)
        for part in range(SPAN):
            for head in range(PARTS):
                lanes = pl.ds((part * PARTS + head) * HD, HD)
                held_ref[rows, lanes] = in_ref[window * SPAN + part, head]
        copies.append(
            pltpu.make_async_copy(held_ref.at[rows], out_ref.at[rows], sems.at[window])
        )
        copies[-1].start()
    for copy in copies:
        copy.wait()


def paste(pieces):
    return pl.pallas_call(
        paste_kernel,
        in_specs=[VMEM],
        out_specs=ANY,
        out_shape=jax.ShapeDtypeStruct((POS, HEADS * HD), jnp.bfloat16),
        scratch_shapes=[
            pltpu.VMEM((POS, HEADS * HD), jnp.bfloat16),
            pltpu.SemaphoreType.DMA((NWIN,)),
        ],
        compiler_params=PARAMS,
        name="paste",
    )(pieces)


def body(query_vectors, key_vectors, value_vectors, chosen_groups, chosen_count):
    group_devices = lax.axis_size("grp")

    def to_peers(block):
        return lax.all_to_all(block, "ctx", split_axis=0, concat_axis=0, tiled=True)

    def up(block):
        return lax.ppermute(block, "grp", [(at, at + 1) for at in range(group_devices - 1)])

    def down(block):
        return lax.ppermute(block, "grp", [(at + 1, at) for at in range(group_devices - 1)])

    later_query = down(query_vectors)
    first, last = cut_first(key_vectors, value_vectors)
    last_up = up(last)
    first = to_peers(first)
    first_up = up(first)
    flags = make_flags(chosen_groups, chosen_count)
    second = to_peers(gate(ANY, cut(later_query, last_up, 10**11), first, flags))
    third = to_peers(gate(HBM, cut_out(query_vectors, last), second))
    ahead_b = attend_ahead(flags, 1, 1, second, 2, second, 3)
    far_b = up(ahead_b)
    far_a = up(attend_ahead(flags, 2, 4, second, 0, first_up, 0, ahead_b))
    merged = attend_near_merged(flags, third, 2, third, 3, second, 3, far_b)
    near, logs = attend_near(flags, 2, third, 0, first, 0, first_up, 0)
    return paste(to_peers(merge(flags, near, logs, far_a, merged)))


def solution(mesh):
    in_specs = (P(("grp", "ctx"), None), P(("grp", "ctx"), None), P(("grp", "ctx"), None), P(), P())
    out_specs = P(("grp", "ctx"), None)
    return jax.shard_map(body, mesh=mesh, in_specs=in_specs, out_specs=out_specs, check_vma=False)
```

```python
import functools
import math

import jax
import jax.numpy as jnp
from jax import lax
from jax.experimental import pallas as pl
from jax.experimental.pallas import tpu as pltpu
from jax.sharding import PartitionSpec as P

HEADS = 12
HD = 128
POS = 256
SPAN = 4
NWIN = 8
LOOK = 2
QB = 256
PARTS = HEADS // SPAN
POSITIONS = POS // NWIN
STAT_ROWS = 32
LOG2E = math.log2(math.e)
FACTOR = HD**-0.5 * LOG2E
NEG_FILL = -1e30
SMEM = pl.BlockSpec(memory_space=pltpu.SMEM)
VMEM = pl.BlockSpec(memory_space=pltpu.VMEM)
ANY = pl.BlockSpec(memory_space=pl.ANY)
HBM = pl.BlockSpec(memory_space=pltpu.HBM)
SMALL = pltpu.CompilerParams(vmem_limit_bytes=2**20)
PARAMS = pltpu.CompilerParams(vmem_limit_bytes=10 * 2**20)


def is_taken(groups_ref, count_ref, group, distance):
    groups = groups_ref.shape[0]
    window = lax.axis_index("ctx") // SPAN
    held = jnp.minimum(group, groups - 1)
    source = group - distance
    count = count_ref[held, window]
    taken = jnp.bool_(False)
    for slot in range(LOOK):
        taken = taken | ((groups_ref[held, window, slot] == source) & (slot < count))
    return taken & (source >= 0) & (group < groups)


def flags_kernel(groups_ref, count_ref, out_ref):
    group = lax.axis_index("grp")
    for at, (owner, distance) in enumerate(((group, 1), (group, 2), (group + 1, 2))):
        out_ref[at] = is_taken(groups_ref, count_ref, owner, distance).astype(jnp.int32)
    out_ref[3] = jnp.int32(0)


def make_flags(groups, count):
    return pl.pallas_call(
        flags_kernel,
        in_specs=[SMEM] * 2,
        out_specs=SMEM,
        out_shape=jax.ShapeDtypeStruct((4,), jnp.int32),
        compiler_params=SMALL,
        name="flags",
    )(groups, count)


def score(query, keys):
    return lax.dot_general(
        query, keys, (((1,), (1,)), ((), ())), preferred_element_type=jnp.float32
    )


def soften(scores, values, diagonal=False):
    if diagonal:
        rows, count = scores.shape
        tail = scores[:, count - rows :]
        frame_query = lax.broadcasted_iota(jnp.int32, (rows, rows), 0) // POSITIONS
        frame_key = lax.broadcasted_iota(jnp.int32, (rows, rows), 1) // POSITIONS
        tail = jnp.where(frame_query >= frame_key, tail, NEG_FILL)
        scores = jnp.concatenate([scores[:, : count - rows], tail], axis=1) if count > rows else tail
    highest = jnp.max(scores, axis=-1, keepdims=True)
    weights = jnp.exp2((scores - highest) * FACTOR)
    beside = jnp.concatenate([values, jnp.ones_like(values)], axis=1)
    product = jnp.dot(weights.astype(jnp.bfloat16), beside, preferred_element_type=jnp.float32)
    return highest, product[:, HD:], product[:, :HD]


def in_turn(jobs, done):
    scores = jobs[0][0]()
    for at, (_, finish) in enumerate(jobs):
        following = jobs[at + 1][0]() if at + 1 < len(jobs) else None
        done(at, finish(scores))
        scores = following


def join(old, new):
    ceiling = jnp.maximum(old[0], new[0])
    old_scale = jnp.exp2((old[0] - ceiling) * FACTOR)
    new_scale = jnp.exp2((new[0] - ceiling) * FACTOR)
    return (
        ceiling,
        old[1] * old_scale + new[1] * new_scale,
        old[2] * old_scale + new[2] * new_scale,
    )


def rows_of(ref, slab, start, size):
    first, count = start // POSITIONS, size // POSITIONS
    return ref[pl.ds(first, count), slab].reshape(size, HD)


def eye_mask():
    return lax.broadcasted_iota(jnp.int32, (HD, HD), 0) == lax.broadcasted_iota(
        jnp.int32, (HD, HD), 1
    )


def log_rows(part):
    log_sum = part[0] * FACTOR + jnp.log(part[1]) * LOG2E
    return [
        jnp.sum(jnp.where(eye_mask(), log_sum[at : at + HD], 0.0), axis=0, keepdims=True)
        for at in range(0, log_sum.shape[0], HD)
    ]


def ahead_kernel(query_slab, pair_slab, flags_ref, q_ref, kv_ref, *rest):
    out_ref = rest[-1]
    rows = q_ref.shape[0] * POSITIONS
    heads = out_ref.shape[0]
    taken = flags_ref[2] > 0

    @pl.when(taken)
    def _():
        @pl.loop(0, heads)
        def _(head):
            keys = kv_ref[:, pair_slab + 2 * head].reshape(rows, HD)
            values = kv_ref[:, pair_slab + 2 * head + 1].reshape(rows, HD)

            def job(start):
                return (
                    lambda: score(rows_of(q_ref, query_slab + head, start, QB), keys),
                    lambda scores: soften(scores, values),
                )

            logs = []

            def done(at, part):
                out_ref[head, pl.ds(at * QB, QB), :] = (part[2] / part[1]).astype(jnp.bfloat16)
                logs.extend(log_rows(part))

            in_turn([job(start) for start in range(0, rows, QB)], done)
            left = jnp.concatenate(logs, axis=0)
            pieces = []
            for _ in range(3):
                pieces.append(left.astype(jnp.bfloat16).astype(jnp.float32))
                left = left - pieces[-1]
            pieces.append(jnp.zeros((STAT_ROWS - 3 * left.shape[0], HD), jnp.float32))
            packed = jnp.concatenate(pieces, axis=0).astype(jnp.bfloat16)
            out_ref[head, pl.ds(rows, STAT_ROWS), :] = packed

    @pl.when(jnp.logical_not(taken))
    def _():
        out_ref[:, pl.ds(rows, STAT_ROWS), :] = jnp.zeros((heads, STAT_ROWS, HD), jnp.bfloat16)


def near_kernel(query_slab, own_slab, up_slab, flags_ref, q_ref, own_ref, up_ref, out_ref, log_ref):
    rows = q_ref.shape[0] * POSITIONS
    heads = out_ref.shape[0]
    taken = flags_ref[0] > 0

    def run(with_earlier):
        @pl.loop(0, heads)
        def _(head):
            def own(start):
                def begin():
                    query = rows_of(q_ref, query_slab + head, start, QB)
                    return score(query, rows_of(own_ref, own_slab + 2 * head, 0, start + QB))

                def finish(scores):
                    return soften(scores, rows_of(own_ref, own_slab + 2 * head + 1, 0, start + QB), True)

                return begin, finish

            def earlier(start):
                def begin():
                    query = rows_of(q_ref, query_slab + head, start, QB)
                    return score(query, rows_of(up_ref, up_slab + 2 * head, 0, rows))

                def finish(scores):
                    return soften(scores, rows_of(up_ref, up_slab + 2 * head + 1, 0, rows))

                return begin, finish

            logs = []
            held = []

            def done(at, part):
                if with_earlier:
                    held.append(part)
                    if at % 2 == 0:
                        return
                    part = join(held[-2], held[-1])
                    at = at // 2
                out_ref[head, pl.ds(at * QB, QB), :] = part[2] / part[1]
                logs.extend(log_rows(part))

            jobs = []
            for start in range(0, rows, QB):
                jobs.append(own(start))
                if with_earlier:
                    jobs.append(earlier(start))
            in_turn(jobs, done)
            log_ref[head] = jnp.concatenate(logs, axis=0)

    @pl.when(taken)
    def _():
        run(True)

    @pl.when(jnp.logical_not(taken))
    def _():
        run(False)


def merge_kernel(flags_ref, near_ref, log_ref, far_ref, *rest):
    out_ref = rest[-1]
    heads, rows, _ = near_ref.shape
    blocks = rows // HD
    taken = flags_ref[1] > 0

    def put(head, block, value):
        count = HD // POSITIONS
        frames = pl.ds(block * count, count)
        out_ref[frames, head] = value.astype(jnp.bfloat16).reshape(count, POSITIONS, HD)

    for other in rest[:-1]:
        out_ref[:, heads:] = other[...]

    @pl.when(taken)
    def _():
        for head in range(heads):
            pieces = far_ref[head, pl.ds(rows, STAT_ROWS), :].astype(jnp.float32)
            far_log = pieces[:blocks] + pieces[blocks : 2 * blocks] + pieces[2 * blocks : 3 * blocks]
            shares = jnp.transpose(1.0 / (1.0 + jnp.exp2(log_ref[head] - far_log)))
            for block in range(blocks):
                part = pl.ds(block * HD, HD)
                near = near_ref[head, part, :]
                far = far_ref[head, part, :].astype(jnp.float32)
                put(head, block, near + (far - near) * shares[:, block : block + 1])

    @pl.when(jnp.logical_not(taken))
    def _():
        for head in range(heads):
            for block in range(blocks):
                put(head, block, near_ref[head, pl.ds(block * HD, HD), :])


def near_merged_kernel(query_slab, own_slab, up_slab, flags_ref, q_ref, own_ref, up_ref, *rest):
    far_ref, out_ref, near_ref, log_ref = rest
    near_kernel(
        query_slab, own_slab, up_slab, flags_ref, q_ref, own_ref, up_ref, near_ref, log_ref
    )
    merge_kernel(flags_ref, near_ref, log_ref, far_ref, out_ref)


def cost(passes, rows, heads, moved):
    return pl.CostEstimate(
        flops=int(4 * passes * rows * rows * heads * HD),
        bytes_accessed=moved,
        transcendentals=int(passes * rows * rows * heads),
    )


def attend_ahead(flags, heads, passes, query, query_slab, pair, pair_slab, *waited):
    rows = pair.shape[0] * POSITIONS
    return pl.pallas_call(
        functools.partial(ahead_kernel, query_slab, pair_slab),
        in_specs=[SMEM] + [VMEM] * 2 + [ANY] * len(waited),
        out_specs=VMEM,
        out_shape=jax.ShapeDtypeStruct((heads, rows + STAT_ROWS, HD), jnp.bfloat16),
        compiler_params=PARAMS,
        cost_estimate=cost(passes, rows, heads, rows * heads * HD * 8),
        name="ahead",
    )(flags, query, pair, *waited)


def attend_near(flags, heads, query, query_slab, own, own_slab, up, up_slab):
    rows = query.shape[0] * POSITIONS
    return pl.pallas_call(
        functools.partial(near_kernel, query_slab, own_slab, up_slab),
        in_specs=[SMEM] + [VMEM] * 3,
        out_specs=[VMEM] * 2,
        out_shape=[
            jax.ShapeDtypeStruct((heads, rows, HD), jnp.float32),
            jax.ShapeDtypeStruct((heads, rows // HD, HD), jnp.float32),
        ],
        compiler_params=PARAMS,
        cost_estimate=cost(160, rows, heads, rows * heads * HD * 14),
        name="near",
    )(flags, query, own, up)


def attend_near_merged(flags, query, query_slab, own, own_slab, up, up_slab, far):
    frames = query.shape[0]
    rows = frames * POSITIONS
    return pl.pallas_call(
        functools.partial(near_merged_kernel, query_slab, own_slab, up_slab),
        in_specs=[SMEM] + [VMEM] * 4,
        out_specs=VMEM,
        out_shape=jax.ShapeDtypeStruct((frames, 1, POSITIONS, HD), jnp.bfloat16),
        scratch_shapes=[
            pltpu.VMEM((1, rows, HD), jnp.float32),
            pltpu.VMEM((1, rows // HD, HD), jnp.float32),
        ],
        compiler_params=PARAMS,
        cost_estimate=cost(1.6, rows, 1, rows * HD * 14),
        name="near_merged",
    )(flags, query, own, up, far)


def merge(flags, near, logs, far, *others):
    heads, rows, _ = near.shape
    slabs = heads + sum(other.shape[1] for other in others)
    return pl.pallas_call(
        merge_kernel,
        in_specs=[SMEM] + [VMEM] * (3 + len(others)),
        out_specs=VMEM,
        out_shape=jax.ShapeDtypeStruct((rows // POSITIONS, slabs, POSITIONS, HD), jnp.bfloat16),
        compiler_params=PARAMS,
        cost_estimate=cost(0, rows, heads, rows * heads * HD * 8),
        name="merge",
    )(flags, near, logs, far, *others)


def cut_first_kernel(k_ref, v_ref, first_ref, last_ref, held_ref, first_piece, last_piece, *sems):
    in_sems, first_sems, last_sems = sems

    def fetch(which, window):
        rows = pl.ds(window * POSITIONS, POSITIONS)
        ref = (k_ref, v_ref)[which]
        return pltpu.make_async_copy(
            ref.at[rows], held_ref.at[which, rows], in_sems.at[which, window]
        )

    def stores(window):
        peers = pl.ds(window * SPAN, SPAN)
        return (
            pltpu.make_async_copy(first_piece.at[peers], first_ref.at[peers], first_sems.at[window]),
            pltpu.make_async_copy(last_piece.at[peers], last_ref.at[peers], last_sems.at[window]),
        )

    for window in range(NWIN):
        for which in range(2):
            fetch(which, window).start()
    for window in range(NWIN):
        rows = pl.ds(window * POSITIONS, POSITIONS)
        for which in range(2):
            fetch(which, window).wait()
            for part in range(SPAN):
                for head in range(PARTS):
                    lanes = pl.ds((part * PARTS + head) * HD, HD)
                    value = held_ref[which, rows, lanes]
                    if head < 2:
                        first_piece[window * SPAN + part, 2 * head + which] = value
                    else:
                        last_piece[window * SPAN + part, which] = value
        for copy in stores(window):
            copy.start()
    for window in range(NWIN):
        for copy in stores(window):
            copy.wait()


def cut_first(key, value):
    first = (NWIN * SPAN, 4, POSITIONS, HD)
    last = (NWIN * SPAN, 2, POSITIONS, HD)
    return pl.pallas_call(
        cut_first_kernel,
        in_specs=[HBM] * 2,
        out_specs=[HBM] * 2,
        out_shape=[jax.ShapeDtypeStruct(shape, jnp.bfloat16) for shape in (first, last)],
        scratch_shapes=[
            pltpu.VMEM((2,) + key.shape, jnp.bfloat16),
            pltpu.VMEM(first, jnp.bfloat16),
            pltpu.VMEM(last, jnp.bfloat16),
            pltpu.SemaphoreType.DMA((2, NWIN)),
            pltpu.SemaphoreType.DMA((NWIN,)),
            pltpu.SemaphoreType.DMA((NWIN,)),
        ],
        compiler_params=pltpu.CompilerParams(vmem_limit_bytes=60 * 2**20),
        name="cut_first",
    )(key, value)


def gate_kernel(*refs):
    del refs


def gate(space, passed, *waited):
    return pl.pallas_call(
        gate_kernel,
        in_specs=[space] + [ANY] * len(waited),
        out_specs=space,
        out_shape=jax.ShapeDtypeStruct(passed.shape, passed.dtype),
        input_output_aliases={0: 0},
        compiler_params=SMALL,
        name="gate",
    )(passed, *waited)


def cut_kernel(whole_ref, piece_ref, out_ref):
    heads = out_ref.shape[1] - piece_ref.shape[1]
    for window in range(NWIN):
        rows = pl.ds(window * POSITIONS, POSITIONS)
        for part in range(SPAN):
            for head in range(heads):
                lanes = pl.ds((part * PARTS + head) * HD, HD)
                out_ref[window * SPAN + part, head] = whole_ref[rows, lanes]
    out_ref[:, heads:] = piece_ref[...]


def cut(whole, piece, flops):
    slabs = PARTS + piece.shape[1]
    return pl.pallas_call(
        cut_kernel,
        in_specs=[VMEM] * 2,
        out_specs=VMEM,
        out_shape=jax.ShapeDtypeStruct((NWIN * SPAN, slabs, POSITIONS, HD), jnp.bfloat16),
        compiler_params=PARAMS,
        cost_estimate=pl.CostEstimate(flops=flops, bytes_accessed=2**21, transcendentals=0),
        name="cut",
    )(whole, piece)


def cut_out_kernel(whole_ref, piece_ref, out_ref, held_ref, sem):
    cut_kernel(whole_ref, piece_ref, held_ref)
    copy = pltpu.make_async_copy(held_ref, out_ref, sem)
    copy.start()
    copy.wait()


def cut_out(whole, piece):
    shape = (NWIN * SPAN, PARTS + piece.shape[1], POSITIONS, HD)
    return pl.pallas_call(
        cut_out_kernel,
        in_specs=[VMEM] * 2,
        out_specs=HBM,
        out_shape=jax.ShapeDtypeStruct(shape, jnp.bfloat16),
        scratch_shapes=[pltpu.VMEM(shape, jnp.bfloat16), pltpu.SemaphoreType.DMA],
        compiler_params=PARAMS,
        cost_estimate=pl.CostEstimate(flops=10**6, bytes_accessed=2**21, transcendentals=0),
        name="cut_out",
    )(whole, piece)


def paste_kernel(in_ref, out_ref, held_ref, sems):
    copies = []
    for window in range(NWIN):
        rows = pl.ds(window * POSITIONS, POSITIONS)
        for part in range(SPAN):
            for head in range(PARTS):
                lanes = pl.ds((part * PARTS + head) * HD, HD)
                held_ref[rows, lanes] = in_ref[window * SPAN + part, head]
        copies.append(
            pltpu.make_async_copy(held_ref.at[rows], out_ref.at[rows], sems.at[window])
        )
        copies[-1].start()
    for copy in copies:
        copy.wait()


def paste(pieces):
    return pl.pallas_call(
        paste_kernel,
        in_specs=[VMEM],
        out_specs=ANY,
        out_shape=jax.ShapeDtypeStruct((POS, HEADS * HD), jnp.bfloat16),
        scratch_shapes=[
            pltpu.VMEM((POS, HEADS * HD), jnp.bfloat16),
            pltpu.SemaphoreType.DMA((NWIN,)),
        ],
        compiler_params=PARAMS,
        name="paste",
    )(pieces)


def body(query_vectors, key_vectors, value_vectors, chosen_groups, chosen_count):
    group_devices = lax.axis_size("grp")

    def to_peers(block):
        return lax.all_to_all(block, "ctx", split_axis=0, concat_axis=0, tiled=True)

    def up(block):
        return lax.ppermute(block, "grp", [(at, at + 1) for at in range(group_devices - 1)])

    def down(block):
        return lax.ppermute(block, "grp", [(at + 1, at) for at in range(group_devices - 1)])

    later_query = down(query_vectors)
    first, last = cut_first(key_vectors, value_vectors)
    last_up = up(last)
    first = to_peers(first)
    first_up = up(first)
    flags = make_flags(chosen_groups, chosen_count)
    second = to_peers(gate(ANY, cut(later_query, last_up, 10**11), first, flags))
    third = to_peers(gate(HBM, cut_out(query_vectors, last), second))
    ahead_b = attend_ahead(flags, 1, 1, second, 2, second, 3)
    far_b = up(ahead_b)
    far_a = up(attend_ahead(flags, 2, 4, second, 0, first_up, 0, ahead_b))
    merged = attend_near_merged(flags, third, 2, third, 3, second, 3, far_b)
    near, logs = attend_near(flags, 2, third, 0, first, 0, first_up, 0)
    return paste(to_peers(merge(flags, near, logs, far_a, merged)))


def solution(mesh):
    in_specs = (P(("grp", "ctx"), None), P(("grp", "ctx"), None), P(("grp", "ctx"), None), P(), P())
    out_specs = P(("grp", "ctx"), None)
    return jax.shard_map(body, mesh=mesh, in_specs=in_specs, out_specs=out_specs, check_vma=False)
```

```python
import functools
import math

import jax
import jax.numpy as jnp
from jax import lax
from jax.experimental import pallas as pl
from jax.experimental.pallas import tpu as pltpu
from jax.sharding import PartitionSpec as P

HEADS = 12
HD = 128
POS = 256
SPAN = 4
NWIN = 8
LOOK = 2
QB = 256
PARTS = HEADS // SPAN
POSITIONS = POS // NWIN
STAT_ROWS = 32
LOG2E = math.log2(math.e)
FACTOR = HD**-0.5 * LOG2E
NEG_FILL = -1e30
SMEM = pl.BlockSpec(memory_space=pltpu.SMEM)
VMEM = pl.BlockSpec(memory_space=pltpu.VMEM)
ANY = pl.BlockSpec(memory_space=pl.ANY)
HBM = pl.BlockSpec(memory_space=pltpu.HBM)
SMALL = pltpu.CompilerParams(vmem_limit_bytes=2**20)
PARAMS = pltpu.CompilerParams(vmem_limit_bytes=10 * 2**20)


def is_taken(groups_ref, count_ref, group, distance):
    groups = groups_ref.shape[0]
    window = lax.axis_index("ctx") // SPAN
    held = jnp.minimum(group, groups - 1)
    source = group - distance
    count = count_ref[held, window]
    taken = jnp.bool_(False)
    for slot in range(LOOK):
        taken = taken | ((groups_ref[held, window, slot] == source) & (slot < count))
    return taken & (source >= 0) & (group < groups)


def flags_kernel(groups_ref, count_ref, out_ref):
    group = lax.axis_index("grp")
    for at, (owner, distance) in enumerate(((group, 1), (group, 2), (group + 1, 2))):
        out_ref[at] = is_taken(groups_ref, count_ref, owner, distance).astype(jnp.int32)
    out_ref[3] = jnp.int32(0)


def make_flags(groups, count):
    return pl.pallas_call(
        flags_kernel,
        in_specs=[SMEM] * 2,
        out_specs=SMEM,
        out_shape=jax.ShapeDtypeStruct((4,), jnp.int32),
        compiler_params=SMALL,
        name="flags",
    )(groups, count)


def score(query, keys):
    return lax.dot_general(
        query, keys, (((1,), (1,)), ((), ())), preferred_element_type=jnp.float32
    )


def soften(scores, values, diagonal=False):
    if diagonal:
        rows, count = scores.shape
        tail = scores[:, count - rows :]
        frame_query = lax.broadcasted_iota(jnp.int32, (rows, rows), 0) // POSITIONS
        frame_key = lax.broadcasted_iota(jnp.int32, (rows, rows), 1) // POSITIONS
        tail = jnp.where(frame_query >= frame_key, tail, NEG_FILL)
        scores = jnp.concatenate([scores[:, : count - rows], tail], axis=1) if count > rows else tail
    highest = jnp.max(scores, axis=-1, keepdims=True)
    weights = jnp.exp2((scores - highest) * FACTOR)
    beside = jnp.concatenate([values, jnp.ones_like(values)], axis=1)
    product = jnp.dot(weights.astype(jnp.bfloat16), beside, preferred_element_type=jnp.float32)
    return highest, product[:, HD:], product[:, :HD]


def in_turn(jobs, done):
    scores = jobs[0][0]()
    for at, (_, finish) in enumerate(jobs):
        following = jobs[at + 1][0]() if at + 1 < len(jobs) else None
        done(at, finish(scores))
        scores = following


def join(old, new):
    ceiling = jnp.maximum(old[0], new[0])
    old_scale = jnp.exp2((old[0] - ceiling) * FACTOR)
    new_scale = jnp.exp2((new[0] - ceiling) * FACTOR)
    return (
        ceiling,
        old[1] * old_scale + new[1] * new_scale,
        old[2] * old_scale + new[2] * new_scale,
    )


def rows_of(ref, slab, start, size):
    first, count = start // POSITIONS, size // POSITIONS
    return ref[pl.ds(first, count), slab].reshape(size, HD)


def eye_mask():
    return lax.broadcasted_iota(jnp.int32, (HD, HD), 0) == lax.broadcasted_iota(
        jnp.int32, (HD, HD), 1
    )


def log_rows(part):
    log_sum = part[0] * FACTOR + jnp.log(part[1]) * LOG2E
    return [
        jnp.sum(jnp.where(eye_mask(), log_sum[at : at + HD], 0.0), axis=0, keepdims=True)
        for at in range(0, log_sum.shape[0], HD)
    ]


def ahead_kernel(query_slab, pair_slab, flags_ref, q_ref, kv_ref, *rest):
    out_ref = rest[-1]
    rows = q_ref.shape[0] * POSITIONS
    heads = out_ref.shape[0]
    taken = flags_ref[2] > 0

    @pl.when(taken)
    def _():
        @pl.loop(0, heads)
        def _(head):
            keys = kv_ref[:, pair_slab + 2 * head].reshape(rows, HD)
            values = kv_ref[:, pair_slab + 2 * head + 1].reshape(rows, HD)

            def job(start):
                return (
                    lambda: score(rows_of(q_ref, query_slab + head, start, QB), keys),
                    lambda scores: soften(scores, values),
                )

            logs = []

            def done(at, part):
                out_ref[head, pl.ds(at * QB, QB), :] = (part[2] / part[1]).astype(jnp.bfloat16)
                logs.extend(log_rows(part))

            in_turn([job(start) for start in range(0, rows, QB)], done)
            left = jnp.concatenate(logs, axis=0)
            pieces = []
            for _ in range(3):
                pieces.append(left.astype(jnp.bfloat16).astype(jnp.float32))
                left = left - pieces[-1]
            pieces.append(jnp.zeros((STAT_ROWS - 3 * left.shape[0], HD), jnp.float32))
            packed = jnp.concatenate(pieces, axis=0).astype(jnp.bfloat16)
            out_ref[head, pl.ds(rows, STAT_ROWS), :] = packed

    @pl.when(jnp.logical_not(taken))
    def _():
        out_ref[:, pl.ds(rows, STAT_ROWS), :] = jnp.zeros((heads, STAT_ROWS, HD), jnp.bfloat16)


def near_kernel(flags_ref, third_ref, second_ref, first_hbm, up_hbm, far_ref, *rest):
    out_ref, log_ref, last_ref, first_ref, up_ref, last_near, last_log, sems = rest
    frames = third_ref.shape[0]
    rows = frames * POSITIONS
    taken = flags_ref[0] > 0
    half = frames // 2
    copies = [
        pltpu.make_async_copy(
            source.at[pl.ds(at * half, half)], held.at[pl.ds(at * half, half)], sems.at[which, at]
        )
        for which, (source, held) in enumerate(((first_hbm, first_ref), (up_hbm, up_ref)))
        for at in range(2)
    ]
    for copy in copies:
        copy.start()

    def run(with_earlier, query_slab, own, up, near_ref, logs_ref, head):
        def job(pair, slab, start, count, diagonal):
            def begin():
                query = rows_of(third_ref, query_slab, start, QB)
                return score(query, rows_of(pair, slab, 0, count))

            def finish(scores):
                return soften(scores, rows_of(pair, slab + 1, 0, count), diagonal)

            return begin, finish

        logs = []
        held = []

        def done(at, part):
            if with_earlier:
                held.append(part)
                if at % 2 == 0:
                    return
                part = join(held[-2], held[-1])
                at = at // 2
            near_ref[head, pl.ds(at * QB, QB), :] = part[2] / part[1]
            logs.extend(log_rows(part))

        jobs = []
        for start in range(0, rows, QB):
            jobs.append(job(own[0], own[1], start, start + QB, True))
            if with_earlier:
                jobs.append(job(up[0], up[1], start, rows, False))
        in_turn(jobs, done)
        logs_ref[head] = jnp.concatenate(logs, axis=0)

    def run_as_taken(*where):
        @pl.when(taken)
        def _():
            run(True, *where)

        @pl.when(jnp.logical_not(taken))
        def _():
            run(False, *where)

    run_as_taken(PARTS - 1, (third_ref, PARTS), (second_ref, PARTS), last_near, last_log, 0)
    merge_kernel(flags_ref, last_near, last_log, far_ref, last_ref)
    for copy in copies:
        copy.wait()

    @pl.loop(0, PARTS - 1)
    def _(head):
        run_as_taken(head, (first_ref, 2 * head), (up_ref, 2 * head), out_ref, log_ref, head)


def merge_kernel(flags_ref, near_ref, log_ref, far_ref, *rest):
    out_ref = rest[-1]
    heads, rows, _ = near_ref.shape
    blocks = rows // HD
    taken = flags_ref[1] > 0

    def put(head, block, value):
        count = HD // POSITIONS
        frames = pl.ds(block * count, count)
        out_ref[frames, head] = value.astype(jnp.bfloat16).reshape(count, POSITIONS, HD)

    for other in rest[:-1]:
        out_ref[:, heads:] = other[...]

    @pl.when(taken)
    def _():
        for head in range(heads):
            pieces = far_ref[head, pl.ds(rows, STAT_ROWS), :].astype(jnp.float32)
            far_log = pieces[:blocks] + pieces[blocks : 2 * blocks] + pieces[2 * blocks : 3 * blocks]
            shares = jnp.transpose(1.0 / (1.0 + jnp.exp2(log_ref[head] - far_log)))
            for block in range(blocks):
                part = pl.ds(block * HD, HD)
                near = near_ref[head, part, :]
                far = far_ref[head, part, :].astype(jnp.float32)
                put(head, block, near + (far - near) * shares[:, block : block + 1])

    @pl.when(jnp.logical_not(taken))
    def _():
        for head in range(heads):
            for block in range(blocks):
                put(head, block, near_ref[head, pl.ds(block * HD, HD), :])


def cost(passes, rows, heads, moved):
    return pl.CostEstimate(
        flops=int(4 * passes * rows * rows * heads * HD),
        bytes_accessed=moved,
        transcendentals=int(passes * rows * rows * heads),
    )


def attend_ahead(flags, heads, passes, query, query_slab, pair, pair_slab, *waited):
    rows = pair.shape[0] * POSITIONS
    return pl.pallas_call(
        functools.partial(ahead_kernel, query_slab, pair_slab),
        in_specs=[SMEM] + [VMEM] * 2 + [ANY] * len(waited),
        out_specs=VMEM,
        out_shape=jax.ShapeDtypeStruct((heads, rows + STAT_ROWS, HD), jnp.bfloat16),
        compiler_params=PARAMS,
        cost_estimate=cost(passes, rows, heads, rows * heads * HD * 8),
        name="ahead",
    )(flags, query, pair, *waited)


def attend_near(flags, third, second, first, first_up, far):
    frames, heads = third.shape[0], PARTS - 1
    rows = frames * POSITIONS
    return pl.pallas_call(
        near_kernel,
        in_specs=[SMEM] + [VMEM] * 2 + [ANY] * 2 + [VMEM],
        out_specs=[VMEM] * 3,
        out_shape=[
            jax.ShapeDtypeStruct((heads, rows, HD), jnp.float32),
            jax.ShapeDtypeStruct((heads, rows // HD, HD), jnp.float32),
            jax.ShapeDtypeStruct((frames, 1, POSITIONS, HD), jnp.bfloat16),
        ],
        scratch_shapes=[
            pltpu.VMEM(first.shape, first.dtype),
            pltpu.VMEM(first_up.shape, first_up.dtype),
            pltpu.VMEM((1, rows, HD), jnp.float32),
            pltpu.VMEM((1, rows // HD, HD), jnp.float32),
            pltpu.SemaphoreType.DMA((2, 2)),
        ],
        compiler_params=pltpu.CompilerParams(vmem_limit_bytes=14 * 2**20),
        cost_estimate=cost(160, rows, heads, rows * heads * HD * 14),
        name="near",
    )(flags, third, second, first, first_up, far)


def merge(flags, near, logs, far, *others):
    heads, rows, _ = near.shape
    slabs = heads + sum(other.shape[1] for other in others)
    return pl.pallas_call(
        merge_kernel,
        in_specs=[SMEM] + [VMEM] * (3 + len(others)),
        out_specs=VMEM,
        out_shape=jax.ShapeDtypeStruct((rows // POSITIONS, slabs, POSITIONS, HD), jnp.bfloat16),
        compiler_params=PARAMS,
        cost_estimate=cost(0, rows, heads, rows * heads * HD * 8),
        name="merge",
    )(flags, near, logs, far, *others)


def cut_first_kernel(k_ref, v_ref, first_ref, last_ref, held_ref, first_piece, last_piece, *sems):
    in_sems, first_sems, last_sems = sems

    def fetch(which, window):
        rows = pl.ds(window * POSITIONS, POSITIONS)
        ref = (k_ref, v_ref)[which]
        return pltpu.make_async_copy(
            ref.at[rows], held_ref.at[which, rows], in_sems.at[which, window]
        )

    def stores(window):
        peers = pl.ds(window * SPAN, SPAN)
        return (
            pltpu.make_async_copy(first_piece.at[peers], first_ref.at[peers], first_sems.at[window]),
            pltpu.make_async_copy(last_piece.at[peers], last_ref.at[peers], last_sems.at[window]),
        )

    for window in range(NWIN):
        for which in range(2):
            fetch(which, window).start()
    for window in range(NWIN):
        rows = pl.ds(window * POSITIONS, POSITIONS)
        for which in range(2):
            fetch(which, window).wait()
            for part in range(SPAN):
                for head in range(PARTS):
                    lanes = pl.ds((part * PARTS + head) * HD, HD)
                    value = held_ref[which, rows, lanes]
                    if head < 2:
                        first_piece[window * SPAN + part, 2 * head + which] = value
                    else:
                        last_piece[window * SPAN + part, which] = value
        for copy in stores(window):
            copy.start()
    for window in range(NWIN):
        for copy in stores(window):
            copy.wait()


def cut_first(key, value):
    first = (NWIN * SPAN, 4, POSITIONS, HD)
    last = (NWIN * SPAN, 2, POSITIONS, HD)
    return pl.pallas_call(
        cut_first_kernel,
        in_specs=[HBM] * 2,
        out_specs=[HBM] * 2,
        out_shape=[jax.ShapeDtypeStruct(shape, jnp.bfloat16) for shape in (first, last)],
        scratch_shapes=[
            pltpu.VMEM((2,) + key.shape, jnp.bfloat16),
            pltpu.VMEM(first, jnp.bfloat16),
            pltpu.VMEM(last, jnp.bfloat16),
            pltpu.SemaphoreType.DMA((2, NWIN)),
            pltpu.SemaphoreType.DMA((NWIN,)),
            pltpu.SemaphoreType.DMA((NWIN,)),
        ],
        compiler_params=pltpu.CompilerParams(vmem_limit_bytes=60 * 2**20),
        name="cut_first",
    )(key, value)


def gate_kernel(*refs):
    del refs


def gate(space, passed, *waited):
    return pl.pallas_call(
        gate_kernel,
        in_specs=[space] + [ANY] * len(waited),
        out_specs=space,
        out_shape=jax.ShapeDtypeStruct(passed.shape, passed.dtype),
        input_output_aliases={0: 0},
        compiler_params=SMALL,
        name="gate",
    )(passed, *waited)


def cut_kernel(whole_ref, piece_ref, out_ref):
    heads = out_ref.shape[1] - piece_ref.shape[1]
    for window in range(NWIN):
        rows = pl.ds(window * POSITIONS, POSITIONS)
        for part in range(SPAN):
            for head in range(heads):
                lanes = pl.ds((part * PARTS + head) * HD, HD)
                out_ref[window * SPAN + part, head] = whole_ref[rows, lanes]
    out_ref[:, heads:] = piece_ref[...]


def cut(whole, piece, flops):
    slabs = PARTS + piece.shape[1]
    return pl.pallas_call(
        cut_kernel,
        in_specs=[VMEM] * 2,
        out_specs=VMEM,
        out_shape=jax.ShapeDtypeStruct((NWIN * SPAN, slabs, POSITIONS, HD), jnp.bfloat16),
        compiler_params=PARAMS,
        cost_estimate=pl.CostEstimate(flops=flops, bytes_accessed=2**21, transcendentals=0),
        name="cut",
    )(whole, piece)


def cut_out_kernel(whole_ref, piece_ref, out_ref, held_ref, sem):
    cut_kernel(whole_ref, piece_ref, held_ref)
    copy = pltpu.make_async_copy(held_ref, out_ref, sem)
    copy.start()
    copy.wait()


def cut_out(whole, piece):
    shape = (NWIN * SPAN, PARTS + piece.shape[1], POSITIONS, HD)
    return pl.pallas_call(
        cut_out_kernel,
        in_specs=[VMEM] * 2,
        out_specs=HBM,
        out_shape=jax.ShapeDtypeStruct(shape, jnp.bfloat16),
        scratch_shapes=[pltpu.VMEM(shape, jnp.bfloat16), pltpu.SemaphoreType.DMA],
        compiler_params=PARAMS,
        cost_estimate=pl.CostEstimate(flops=10**6, bytes_accessed=2**21, transcendentals=0),
        name="cut_out",
    )(whole, piece)


def paste_kernel(in_ref, out_ref, held_ref, sems):
    copies = []
    for window in range(NWIN):
        rows = pl.ds(window * POSITIONS, POSITIONS)
        for part in range(SPAN):
            for head in range(PARTS):
                lanes = pl.ds((part * PARTS + head) * HD, HD)
                held_ref[rows, lanes] = in_ref[window * SPAN + part, head]
        copies.append(
            pltpu.make_async_copy(held_ref.at[rows], out_ref.at[rows], sems.at[window])
        )
        copies[-1].start()
    for copy in copies:
        copy.wait()


def paste(pieces):
    return pl.pallas_call(
        paste_kernel,
        in_specs=[VMEM],
        out_specs=ANY,
        out_shape=jax.ShapeDtypeStruct((POS, HEADS * HD), jnp.bfloat16),
        scratch_shapes=[
            pltpu.VMEM((POS, HEADS * HD), jnp.bfloat16),
            pltpu.SemaphoreType.DMA((NWIN,)),
        ],
        compiler_params=PARAMS,
        name="paste",
    )(pieces)


def body(query_vectors, key_vectors, value_vectors, chosen_groups, chosen_count):
    group_devices = lax.axis_size("grp")

    def to_peers(block):
        return lax.all_to_all(block, "ctx", split_axis=0, concat_axis=0, tiled=True)

    def up(block):
        return lax.ppermute(block, "grp", [(at, at + 1) for at in range(group_devices - 1)])

    def down(block):
        return lax.ppermute(block, "grp", [(at + 1, at) for at in range(group_devices - 1)])

    later_query = down(query_vectors)
    first, last = cut_first(key_vectors, value_vectors)
    last_up = up(last)
    first = to_peers(first)
    first_up = up(first)
    flags = make_flags(chosen_groups, chosen_count)
    second = to_peers(gate(ANY, cut(later_query, last_up, 10**11), first, flags))
    third = to_peers(gate(HBM, cut_out(query_vectors, last), second))
    ahead_b = attend_ahead(flags, 1, 1, second, 2, second, 3)
    far_b = up(ahead_b)
    far_a = up(attend_ahead(flags, 2, 4, second, 0, first_up, 0, ahead_b))
    near, logs, merged = attend_near(flags, third, second, first, first_up, far_b)
    return paste(to_peers(merge(flags, near, logs, far_a, merged)))


def solution(mesh):
    in_specs = (P(("grp", "ctx"), None), P(("grp", "ctx"), None), P(("grp", "ctx"), None), P(), P())
    out_specs = P(("grp", "ctx"), None)
    return jax.shard_map(body, mesh=mesh, in_specs=in_specs, out_specs=out_specs, check_vma=False)
```

```python
import functools
import math

import jax
import jax.numpy as jnp
from jax import lax
from jax.experimental import pallas as pl
from jax.experimental.pallas import tpu as pltpu
from jax.sharding import PartitionSpec as P

HEADS = 12
HD = 128
POS = 256
SPAN = 4
NWIN = 8
LOOK = 2
QB = 512
PARTS = HEADS // SPAN
POSITIONS = POS // NWIN
STAT_ROWS = 32
LOG2E = math.log2(math.e)
FACTOR = HD**-0.5 * LOG2E
NEG_FILL = -1e30
SMEM = pl.BlockSpec(memory_space=pltpu.SMEM)
VMEM = pl.BlockSpec(memory_space=pltpu.VMEM)
ANY = pl.BlockSpec(memory_space=pl.ANY)
HBM = pl.BlockSpec(memory_space=pltpu.HBM)
SMALL = pltpu.CompilerParams(vmem_limit_bytes=2**20)
PARAMS = pltpu.CompilerParams(vmem_limit_bytes=16 * 2**20)


def is_taken(groups_ref, count_ref, group, distance):
    groups = groups_ref.shape[0]
    window = lax.axis_index("ctx") // SPAN
    held = jnp.minimum(group, groups - 1)
    source = group - distance
    count = count_ref[held, window]
    taken = jnp.bool_(False)
    for slot in range(LOOK):
        taken = taken | ((groups_ref[held, window, slot] == source) & (slot < count))
    return taken & (source >= 0) & (group < groups)


def flags_kernel(groups_ref, count_ref, out_ref):
    group = lax.axis_index("grp")
    for at, (owner, distance) in enumerate(((group, 1), (group, 2), (group + 1, 2))):
        out_ref[at] = is_taken(groups_ref, count_ref, owner, distance).astype(jnp.int32)
    out_ref[3] = jnp.int32(0)


def make_flags(groups, count):
    return pl.pallas_call(
        flags_kernel,
        in_specs=[SMEM] * 2,
        out_specs=SMEM,
        out_shape=jax.ShapeDtypeStruct((4,), jnp.int32),
        compiler_params=SMALL,
        name="flags",
    )(groups, count)


def score(query, keys):
    return lax.dot_general(
        query, keys, (((1,), (1,)), ((), ())), preferred_element_type=jnp.float32
    )


def soften(scores, values, diagonal=False):
    if diagonal:
        rows, count = scores.shape
        tail = scores[:, count - rows :]
        frame_query = lax.broadcasted_iota(jnp.int32, (rows, rows), 0) // POSITIONS
        frame_key = lax.broadcasted_iota(jnp.int32, (rows, rows), 1) // POSITIONS
        tail = jnp.where(frame_query >= frame_key, tail, NEG_FILL)
        scores = jnp.concatenate([scores[:, : count - rows], tail], axis=1) if count > rows else tail
    highest = jnp.max(scores, axis=-1, keepdims=True)
    weights = jnp.exp2((scores - highest) * FACTOR)
    beside = jnp.concatenate([values, jnp.ones_like(values)], axis=1)
    product = jnp.dot(weights.astype(jnp.bfloat16), beside, preferred_element_type=jnp.float32)
    return highest, product[:, HD:], product[:, :HD]


def in_turn(jobs, done):
    scores = jobs[0][0]()
    for at, (_, finish) in enumerate(jobs):
        following = jobs[at + 1][0]() if at + 1 < len(jobs) else None
        done(at, finish(scores))
        scores = following


def join(old, new):
    ceiling = jnp.maximum(old[0], new[0])
    old_scale = jnp.exp2((old[0] - ceiling) * FACTOR)
    new_scale = jnp.exp2((new[0] - ceiling) * FACTOR)
    return (
        ceiling,
        old[1] * old_scale + new[1] * new_scale,
        old[2] * old_scale + new[2] * new_scale,
    )


def rows_of(ref, slab, start, size):
    first, count = start // POSITIONS, size // POSITIONS
    return ref[pl.ds(first, count), slab].reshape(size, HD)


def eye_mask():
    return lax.broadcasted_iota(jnp.int32, (HD, HD), 0) == lax.broadcasted_iota(
        jnp.int32, (HD, HD), 1
    )


def log_rows(part):
    log_sum = part[0] * FACTOR + jnp.log(part[1]) * LOG2E
    return [
        jnp.sum(jnp.where(eye_mask(), log_sum[at : at + HD], 0.0), axis=0, keepdims=True)
        for at in range(0, log_sum.shape[0], HD)
    ]


def ahead_kernel(query_slab, pair_slab, flags_ref, q_ref, kv_ref, *rest):
    out_ref = rest[-1]
    rows = q_ref.shape[0] * POSITIONS
    heads = out_ref.shape[0]
    taken = flags_ref[2] > 0

    @pl.when(taken)
    def _():
        @pl.loop(0, heads)
        def _(head):
            keys = kv_ref[:, pair_slab + 2 * head].reshape(rows, HD)
            values = kv_ref[:, pair_slab + 2 * head + 1].reshape(rows, HD)

            def job(start):
                return (
                    lambda: score(rows_of(q_ref, query_slab + head, start, QB), keys),
                    lambda scores: soften(scores, values),
                )

            logs = []

            def done(at, part):
                out_ref[head, pl.ds(at * QB, QB), :] = (part[2] / part[1]).astype(jnp.bfloat16)
                logs.extend(log_rows(part))

            in_turn([job(start) for start in range(0, rows, QB)], done)
            left = jnp.concatenate(logs, axis=0)
            pieces = []
            for _ in range(3):
                pieces.append(left.astype(jnp.bfloat16).astype(jnp.float32))
                left = left - pieces[-1]
            pieces.append(jnp.zeros((STAT_ROWS - 3 * left.shape[0], HD), jnp.float32))
            packed = jnp.concatenate(pieces, axis=0).astype(jnp.bfloat16)
            out_ref[head, pl.ds(rows, STAT_ROWS), :] = packed

    @pl.when(jnp.logical_not(taken))
    def _():
        out_ref[:, pl.ds(rows, STAT_ROWS), :] = jnp.zeros((heads, STAT_ROWS, HD), jnp.bfloat16)


def near_kernel(flags_ref, third_ref, second_ref, first_hbm, up_hbm, far_ref, *rest):
    out_ref, log_ref, last_ref, first_ref, up_ref, last_near, last_log, sems = rest
    frames = third_ref.shape[0]
    rows = frames * POSITIONS
    taken = flags_ref[0] > 0
    half = frames // 2
    copies = [
        pltpu.make_async_copy(
            source.at[pl.ds(at * half, half)], held.at[pl.ds(at * half, half)], sems.at[which, at]
        )
        for which, (source, held) in enumerate(((first_hbm, first_ref), (up_hbm, up_ref)))
        for at in range(2)
    ]
    for copy in copies:
        copy.start()

    def run(with_earlier, query_slab, own, up, near_ref, logs_ref, head):
        def job(pair, slab, start, count, diagonal):
            def begin():
                query = rows_of(third_ref, query_slab, start, QB)
                return score(query, rows_of(pair, slab, 0, count))

            def finish(scores):
                return soften(scores, rows_of(pair, slab + 1, 0, count), diagonal)

            return begin, finish

        logs = []
        held = []

        def done(at, part):
            if with_earlier:
                held.append(part)
                if at % 2 == 0:
                    return
                part = join(held[-2], held[-1])
                at = at // 2
            near_ref[head, pl.ds(at * QB, QB), :] = part[2] / part[1]
            logs.extend(log_rows(part))

        jobs = []
        for start in range(0, rows, QB):
            jobs.append(job(own[0], own[1], start, start + QB, True))
            if with_earlier:
                jobs.append(job(up[0], up[1], start, rows, False))
        in_turn(jobs, done)
        logs_ref[head] = jnp.concatenate(logs, axis=0)

    def run_as_taken(*where):
        @pl.when(taken)
        def _():
            run(True, *where)

        @pl.when(jnp.logical_not(taken))
        def _():
            run(False, *where)

    run_as_taken(PARTS - 1, (third_ref, PARTS), (second_ref, PARTS), last_near, last_log, 0)
    merge_kernel(flags_ref, last_near, last_log, far_ref, last_ref)
    for copy in copies:
        copy.wait()

    @pl.loop(0, PARTS - 1)
    def _(head):
        run_as_taken(head, (first_ref, 2 * head), (up_ref, 2 * head), out_ref, log_ref, head)


def merge_kernel(flags_ref, near_ref, log_ref, far_ref, *rest):
    out_ref = rest[-1]
    heads, rows, _ = near_ref.shape
    blocks = rows // HD
    taken = flags_ref[1] > 0

    def put(head, block, value):
        count = HD // POSITIONS
        frames = pl.ds(block * count, count)
        out_ref[frames, head] = value.astype(jnp.bfloat16).reshape(count, POSITIONS, HD)

    for other in rest[:-1]:
        out_ref[:, heads:] = other[...]

    @pl.when(taken)
    def _():
        for head in range(heads):
            pieces = far_ref[head, pl.ds(rows, STAT_ROWS), :].astype(jnp.float32)
            far_log = pieces[:blocks] + pieces[blocks : 2 * blocks] + pieces[2 * blocks : 3 * blocks]
            shares = jnp.transpose(1.0 / (1.0 + jnp.exp2(log_ref[head] - far_log)))
            for block in range(blocks):
                part = pl.ds(block * HD, HD)
                near = near_ref[head, part, :]
                far = far_ref[head, part, :].astype(jnp.float32)
                put(head, block, near + (far - near) * shares[:, block : block + 1])

    @pl.when(jnp.logical_not(taken))
    def _():
        for head in range(heads):
            for block in range(blocks):
                put(head, block, near_ref[head, pl.ds(block * HD, HD), :])


def cost(passes, rows, heads, moved):
    return pl.CostEstimate(
        flops=int(4 * passes * rows * rows * heads * HD),
        bytes_accessed=moved,
        transcendentals=int(passes * rows * rows * heads),
    )


def attend_ahead(flags, heads, passes, query, query_slab, pair, pair_slab, *waited):
    rows = pair.shape[0] * POSITIONS
    return pl.pallas_call(
        functools.partial(ahead_kernel, query_slab, pair_slab),
        in_specs=[SMEM] + [VMEM] * 2 + [ANY] * len(waited),
        out_specs=VMEM,
        out_shape=jax.ShapeDtypeStruct((heads, rows + STAT_ROWS, HD), jnp.bfloat16),
        compiler_params=PARAMS,
        cost_estimate=cost(passes, rows, heads, rows * heads * HD * 8),
        name="ahead",
    )(flags, query, pair, *waited)


def attend_near(flags, third, second, first, first_up, far):
    frames, heads = third.shape[0], PARTS - 1
    rows = frames * POSITIONS
    return pl.pallas_call(
        near_kernel,
        in_specs=[SMEM] + [VMEM] * 2 + [ANY] * 2 + [VMEM],
        out_specs=[VMEM] * 3,
        out_shape=[
            jax.ShapeDtypeStruct((heads, rows, HD), jnp.float32),
            jax.ShapeDtypeStruct((heads, rows // HD, HD), jnp.float32),
            jax.ShapeDtypeStruct((frames, 1, POSITIONS, HD), jnp.bfloat16),
        ],
        scratch_shapes=[
            pltpu.VMEM(first.shape, first.dtype),
            pltpu.VMEM(first_up.shape, first_up.dtype),
            pltpu.VMEM((1, rows, HD), jnp.float32),
            pltpu.VMEM((1, rows // HD, HD), jnp.float32),
            pltpu.SemaphoreType.DMA((2, 2)),
        ],
        compiler_params=pltpu.CompilerParams(vmem_limit_bytes=20 * 2**20),
        cost_estimate=cost(160, rows, heads, rows * heads * HD * 14),
        name="near",
    )(flags, third, second, first, first_up, far)


def merge(flags, near, logs, far, *others):
    heads, rows, _ = near.shape
    slabs = heads + sum(other.shape[1] for other in others)
    return pl.pallas_call(
        merge_kernel,
        in_specs=[SMEM] + [VMEM] * (3 + len(others)),
        out_specs=VMEM,
        out_shape=jax.ShapeDtypeStruct((rows // POSITIONS, slabs, POSITIONS, HD), jnp.bfloat16),
        compiler_params=PARAMS,
        cost_estimate=cost(0, rows, heads, rows * heads * HD * 8),
        name="merge",
    )(flags, near, logs, far, *others)


def cut_first_kernel(k_ref, v_ref, first_ref, last_ref, held_ref, first_piece, last_piece, *sems):
    in_sems, first_sems, last_sems = sems

    def fetch(which, window):
        rows = pl.ds(window * POSITIONS, POSITIONS)
        ref = (k_ref, v_ref)[which]
        return pltpu.make_async_copy(
            ref.at[rows], held_ref.at[which, rows], in_sems.at[which, window]
        )

    def stores(window):
        peers = pl.ds(window * SPAN, SPAN)
        return (
            pltpu.make_async_copy(first_piece.at[peers], first_ref.at[peers], first_sems.at[window]),
            pltpu.make_async_copy(last_piece.at[peers], last_ref.at[peers], last_sems.at[window]),
        )

    for window in range(NWIN):
        for which in range(2):
            fetch(which, window).start()
    for window in range(NWIN):
        rows = pl.ds(window * POSITIONS, POSITIONS)
        for which in range(2):
            fetch(which, window).wait()
            for part in range(SPAN):
                for head in range(PARTS):
                    lanes = pl.ds((part * PARTS + head) * HD, HD)
                    value = held_ref[which, rows, lanes]
                    if head < 2:
                        first_piece[window * SPAN + part, 2 * head + which] = value
                    else:
                        last_piece[window * SPAN + part, which] = value
        for copy in stores(window):
            copy.start()
    for window in range(NWIN):
        for copy in stores(window):
            copy.wait()


def cut_first(key, value):
    first = (NWIN * SPAN, 4, POSITIONS, HD)
    last = (NWIN * SPAN, 2, POSITIONS, HD)
    return pl.pallas_call(
        cut_first_kernel,
        in_specs=[HBM] * 2,
        out_specs=[HBM] * 2,
        out_shape=[jax.ShapeDtypeStruct(shape, jnp.bfloat16) for shape in (first, last)],
        scratch_shapes=[
            pltpu.VMEM((2,) + key.shape, jnp.bfloat16),
            pltpu.VMEM(first, jnp.bfloat16),
            pltpu.VMEM(last, jnp.bfloat16),
            pltpu.SemaphoreType.DMA((2, NWIN)),
            pltpu.SemaphoreType.DMA((NWIN,)),
            pltpu.SemaphoreType.DMA((NWIN,)),
        ],
        compiler_params=pltpu.CompilerParams(vmem_limit_bytes=60 * 2**20),
        name="cut_first",
    )(key, value)


def gate_kernel(*refs):
    del refs


def gate(space, passed, *waited):
    return pl.pallas_call(
        gate_kernel,
        in_specs=[space] + [ANY] * len(waited),
        out_specs=space,
        out_shape=jax.ShapeDtypeStruct(passed.shape, passed.dtype),
        input_output_aliases={0: 0},
        compiler_params=SMALL,
        name="gate",
    )(passed, *waited)


def cut_kernel(whole_ref, piece_ref, out_ref):
    heads = out_ref.shape[1] - piece_ref.shape[1]
    for window in range(NWIN):
        rows = pl.ds(window * POSITIONS, POSITIONS)
        for part in range(SPAN):
            for head in range(heads):
                lanes = pl.ds((part * PARTS + head) * HD, HD)
                out_ref[window * SPAN + part, head] = whole_ref[rows, lanes]
    out_ref[:, heads:] = piece_ref[...]


def cut(whole, piece, flops):
    slabs = PARTS + piece.shape[1]
    return pl.pallas_call(
        cut_kernel,
        in_specs=[VMEM] * 2,
        out_specs=VMEM,
        out_shape=jax.ShapeDtypeStruct((NWIN * SPAN, slabs, POSITIONS, HD), jnp.bfloat16),
        compiler_params=PARAMS,
        cost_estimate=pl.CostEstimate(flops=flops, bytes_accessed=2**21, transcendentals=0),
        name="cut",
    )(whole, piece)


def cut_out_kernel(whole_ref, piece_ref, out_ref, held_ref, sem):
    cut_kernel(whole_ref, piece_ref, held_ref)
    copy = pltpu.make_async_copy(held_ref, out_ref, sem)
    copy.start()
    copy.wait()


def cut_out(whole, piece):
    shape = (NWIN * SPAN, PARTS + piece.shape[1], POSITIONS, HD)
    return pl.pallas_call(
        cut_out_kernel,
        in_specs=[VMEM] * 2,
        out_specs=HBM,
        out_shape=jax.ShapeDtypeStruct(shape, jnp.bfloat16),
        scratch_shapes=[pltpu.VMEM(shape, jnp.bfloat16), pltpu.SemaphoreType.DMA],
        compiler_params=PARAMS,
        cost_estimate=pl.CostEstimate(flops=10**6, bytes_accessed=2**21, transcendentals=0),
        name="cut_out",
    )(whole, piece)


def paste_kernel(in_ref, out_ref, held_ref, sems):
    copies = []
    for window in range(NWIN):
        rows = pl.ds(window * POSITIONS, POSITIONS)
        for part in range(SPAN):
            for head in range(PARTS):
                lanes = pl.ds((part * PARTS + head) * HD, HD)
                held_ref[rows, lanes] = in_ref[window * SPAN + part, head]
        copies.append(
            pltpu.make_async_copy(held_ref.at[rows], out_ref.at[rows], sems.at[window])
        )
        copies[-1].start()
    for copy in copies:
        copy.wait()


def paste(pieces):
    return pl.pallas_call(
        paste_kernel,
        in_specs=[VMEM],
        out_specs=ANY,
        out_shape=jax.ShapeDtypeStruct((POS, HEADS * HD), jnp.bfloat16),
        scratch_shapes=[
            pltpu.VMEM((POS, HEADS * HD), jnp.bfloat16),
            pltpu.SemaphoreType.DMA((NWIN,)),
        ],
        compiler_params=PARAMS,
        name="paste",
    )(pieces)


def body(query_vectors, key_vectors, value_vectors, chosen_groups, chosen_count):
    group_devices = lax.axis_size("grp")

    def to_peers(block):
        return lax.all_to_all(block, "ctx", split_axis=0, concat_axis=0, tiled=True)

    def up(block):
        return lax.ppermute(block, "grp", [(at, at + 1) for at in range(group_devices - 1)])

    def down(block):
        return lax.ppermute(block, "grp", [(at + 1, at) for at in range(group_devices - 1)])

    later_query = down(query_vectors)
    first, last = cut_first(key_vectors, value_vectors)
    last_up = up(last)
    first = to_peers(first)
    first_up = up(first)
    flags = make_flags(chosen_groups, chosen_count)
    second = to_peers(gate(ANY, cut(later_query, last_up, 10**11), first, flags))
    third = to_peers(gate(HBM, cut_out(query_vectors, last), second))
    ahead_b = attend_ahead(flags, 1, 1, second, 2, second, 3)
    far_b = up(ahead_b)
    far_a = up(attend_ahead(flags, 2, 4, second, 0, first_up, 0, ahead_b))
    near, logs, merged = attend_near(flags, third, second, first, first_up, far_b)
    return paste(to_peers(merge(flags, near, logs, far_a, merged)))


def solution(mesh):
    in_specs = (P(("grp", "ctx"), None), P(("grp", "ctx"), None), P(("grp", "ctx"), None), P(), P())
    out_specs = P(("grp", "ctx"), None)
    return jax.shard_map(body, mesh=mesh, in_specs=in_specs, out_specs=out_specs, check_vma=False)
```

```python
import functools
import math

import jax
import jax.numpy as jnp
from jax import lax
from jax.experimental import pallas as pl
from jax.experimental.pallas import tpu as pltpu
from jax.sharding import PartitionSpec as P

HEADS = 12
HD = 128
POS = 256
SPAN = 4
NWIN = 8
LOOK = 2
QB = 256
AHEAD_QB = 512
PARTS = HEADS // SPAN
POSITIONS = POS // NWIN
STAT_ROWS = 32
LOG2E = math.log2(math.e)
FACTOR = HD**-0.5 * LOG2E
NEG_FILL = -1e30
SMEM = pl.BlockSpec(memory_space=pltpu.SMEM)
VMEM = pl.BlockSpec(memory_space=pltpu.VMEM)
ANY = pl.BlockSpec(memory_space=pl.ANY)
HBM = pl.BlockSpec(memory_space=pltpu.HBM)
SMALL = pltpu.CompilerParams(vmem_limit_bytes=2**20)
PARAMS = pltpu.CompilerParams(vmem_limit_bytes=16 * 2**20)


def is_taken(groups_ref, count_ref, group, distance):
    groups = groups_ref.shape[0]
    window = lax.axis_index("ctx") // SPAN
    held = jnp.minimum(group, groups - 1)
    source = group - distance
    count = count_ref[held, window]
    taken = jnp.bool_(False)
    for slot in range(LOOK):
        taken = taken | ((groups_ref[held, window, slot] == source) & (slot < count))
    return taken & (source >= 0) & (group < groups)


def flags_kernel(groups_ref, count_ref, out_ref):
    group = lax.axis_index("grp")
    for at, (owner, distance) in enumerate(((group, 1), (group, 2), (group + 1, 2))):
        out_ref[at] = is_taken(groups_ref, count_ref, owner, distance).astype(jnp.int32)
    out_ref[3] = jnp.int32(0)


def make_flags(groups, count):
    return pl.pallas_call(
        flags_kernel,
        in_specs=[SMEM] * 2,
        out_specs=SMEM,
        out_shape=jax.ShapeDtypeStruct((4,), jnp.int32),
        compiler_params=SMALL,
        name="flags",
    )(groups, count)


def score(query, keys):
    return lax.dot_general(
        query, keys, (((1,), (1,)), ((), ())), preferred_element_type=jnp.float32
    )


def soften(scores, values, diagonal=False):
    if diagonal:
        rows, count = scores.shape
        tail = scores[:, count - rows :]
        frame_query = lax.broadcasted_iota(jnp.int32, (rows, rows), 0) // POSITIONS
        frame_key = lax.broadcasted_iota(jnp.int32, (rows, rows), 1) // POSITIONS
        tail = jnp.where(frame_query >= frame_key, tail, NEG_FILL)
        scores = jnp.concatenate([scores[:, : count - rows], tail], axis=1) if count > rows else tail
    highest = jnp.max(scores, axis=-1, keepdims=True)
    weights = jnp.exp2((scores - highest) * FACTOR)
    beside = jnp.concatenate([values, jnp.ones_like(values)], axis=1)
    product = jnp.dot(weights.astype(jnp.bfloat16), beside, preferred_element_type=jnp.float32)
    return highest, product[:, HD:], product[:, :HD]


def in_turn(jobs, done):
    scores = jobs[0][0]()
    for at, (_, finish) in enumerate(jobs):
        following = jobs[at + 1][0]() if at + 1 < len(jobs) else None
        done(at, finish(scores))
        scores = following


def join(old, new):
    ceiling = jnp.maximum(old[0], new[0])
    old_scale = jnp.exp2((old[0] - ceiling) * FACTOR)
    new_scale = jnp.exp2((new[0] - ceiling) * FACTOR)
    return (
        ceiling,
        old[1] * old_scale + new[1] * new_scale,
        old[2] * old_scale + new[2] * new_scale,
    )


def rows_of(ref, slab, start, size):
    first, count = start // POSITIONS, size // POSITIONS
    return ref[pl.ds(first, count), slab].reshape(size, HD)


def eye_mask():
    return lax.broadcasted_iota(jnp.int32, (HD, HD), 0) == lax.broadcasted_iota(
        jnp.int32, (HD, HD), 1
    )


def log_rows(part):
    log_sum = part[0] * FACTOR + jnp.log(part[1]) * LOG2E
    return [
        jnp.sum(jnp.where(eye_mask(), log_sum[at : at + HD], 0.0), axis=0, keepdims=True)
        for at in range(0, log_sum.shape[0], HD)
    ]


def ahead_kernel(query_slab, pair_slab, flags_ref, q_ref, kv_ref, *rest):
    out_ref = rest[-1]
    rows = q_ref.shape[0] * POSITIONS
    heads = out_ref.shape[0]
    taken = flags_ref[2] > 0

    @pl.when(taken)
    def _():
        @pl.loop(0, heads)
        def _(head):
            keys = kv_ref[:, pair_slab + 2 * head].reshape(rows, HD)
            values = kv_ref[:, pair_slab + 2 * head + 1].reshape(rows, HD)

            def job(start):
                return (
                    lambda: score(rows_of(q_ref, query_slab + head, start, AHEAD_QB), keys),
                    lambda scores: soften(scores, values),
                )

            logs = []

            def done(at, part):
                out_ref[head, pl.ds(at * AHEAD_QB, AHEAD_QB), :] = (part[2] / part[1]).astype(jnp.bfloat16)
                logs.extend(log_rows(part))

            in_turn([job(start) for start in range(0, rows, AHEAD_QB)], done)
            left = jnp.concatenate(logs, axis=0)
            pieces = []
            for _ in range(3):
                pieces.append(left.astype(jnp.bfloat16).astype(jnp.float32))
                left = left - pieces[-1]
            pieces.append(jnp.zeros((STAT_ROWS - 3 * left.shape[0], HD), jnp.float32))
            packed = jnp.concatenate(pieces, axis=0).astype(jnp.bfloat16)
            out_ref[head, pl.ds(rows, STAT_ROWS), :] = packed

    @pl.when(jnp.logical_not(taken))
    def _():
        out_ref[:, pl.ds(rows, STAT_ROWS), :] = jnp.zeros((heads, STAT_ROWS, HD), jnp.bfloat16)


def near_kernel(flags_ref, third_ref, second_ref, first_hbm, up_hbm, far_ref, *rest):
    out_ref, log_ref, last_ref, first_ref, up_ref, last_near, last_log, sems = rest
    frames = third_ref.shape[0]
    rows = frames * POSITIONS
    taken = flags_ref[0] > 0
    half = frames // 2
    copies = [
        pltpu.make_async_copy(
            source.at[pl.ds(at * half, half)], held.at[pl.ds(at * half, half)], sems.at[which, at]
        )
        for which, (source, held) in enumerate(((first_hbm, first_ref), (up_hbm, up_ref)))
        for at in range(2)
    ]
    for copy in copies:
        copy.start()

    def run(with_earlier, query_slab, own, up, near_ref, logs_ref, head):
        def job(pair, slab, start, count, diagonal):
            def begin():
                query = rows_of(third_ref, query_slab, start, QB)
                return score(query, rows_of(pair, slab, 0, count))

            def finish(scores):
                return soften(scores, rows_of(pair, slab + 1, 0, count), diagonal)

            return begin, finish

        logs = []
        held = []

        def done(at, part):
            if with_earlier:
                held.append(part)
                if at % 2 == 0:
                    return
                part = join(held[-2], held[-1])
                at = at // 2
            near_ref[head, pl.ds(at * QB, QB), :] = part[2] / part[1]
            logs.extend(log_rows(part))

        jobs = []
        for start in range(0, rows, QB):
            jobs.append(job(own[0], own[1], start, start + QB, True))
            if with_earlier:
                jobs.append(job(up[0], up[1], start, rows, False))
        in_turn(jobs, done)
        logs_ref[head] = jnp.concatenate(logs, axis=0)

    def run_as_taken(*where):
        @pl.when(taken)
        def _():
            run(True, *where)

        @pl.when(jnp.logical_not(taken))
        def _():
            run(False, *where)

    run_as_taken(PARTS - 1, (third_ref, PARTS), (second_ref, PARTS), last_near, last_log, 0)
    merge_kernel(flags_ref, last_near, last_log, far_ref, last_ref)
    for copy in copies:
        copy.wait()

    @pl.loop(0, PARTS - 1)
    def _(head):
        run_as_taken(head, (first_ref, 2 * head), (up_ref, 2 * head), out_ref, log_ref, head)


def merge_kernel(flags_ref, near_ref, log_ref, far_ref, *rest):
    out_ref = rest[-1]
    heads, rows, _ = near_ref.shape
    blocks = rows // HD
    taken = flags_ref[1] > 0

    def put(head, block, value):
        count = HD // POSITIONS
        frames = pl.ds(block * count, count)
        out_ref[frames, head] = value.astype(jnp.bfloat16).reshape(count, POSITIONS, HD)

    for other in rest[:-1]:
        out_ref[:, heads:] = other[...]

    @pl.when(taken)
    def _():
        for head in range(heads):
            pieces = far_ref[head, pl.ds(rows, STAT_ROWS), :].astype(jnp.float32)
            far_log = pieces[:blocks] + pieces[blocks : 2 * blocks] + pieces[2 * blocks : 3 * blocks]
            shares = jnp.transpose(1.0 / (1.0 + jnp.exp2(log_ref[head] - far_log)))
            for block in range(blocks):
                part = pl.ds(block * HD, HD)
                near = near_ref[head, part, :]
                far = far_ref[head, part, :].astype(jnp.float32)
                put(head, block, near + (far - near) * shares[:, block : block + 1])

    @pl.when(jnp.logical_not(taken))
    def _():
        for head in range(heads):
            for block in range(blocks):
                put(head, block, near_ref[head, pl.ds(block * HD, HD), :])


def cost(passes, rows, heads, moved):
    return pl.CostEstimate(
        flops=int(4 * passes * rows * rows * heads * HD),
        bytes_accessed=moved,
        transcendentals=int(passes * rows * rows * heads),
    )


def attend_ahead(flags, heads, passes, query, query_slab, pair, pair_slab, *waited):
    rows = pair.shape[0] * POSITIONS
    return pl.pallas_call(
        functools.partial(ahead_kernel, query_slab, pair_slab),
        in_specs=[SMEM] + [VMEM] * 2 + [ANY] * len(waited),
        out_specs=VMEM,
        out_shape=jax.ShapeDtypeStruct((heads, rows + STAT_ROWS, HD), jnp.bfloat16),
        compiler_params=PARAMS,
        cost_estimate=cost(passes, rows, heads, rows * heads * HD * 8),
        name="ahead",
    )(flags, query, pair, *waited)


def attend_near(flags, third, second, first, first_up, far):
    frames, heads = third.shape[0], PARTS - 1
    rows = frames * POSITIONS
    return pl.pallas_call(
        near_kernel,
        in_specs=[SMEM] + [VMEM] * 2 + [ANY] * 2 + [VMEM],
        out_specs=[VMEM] * 3,
        out_shape=[
            jax.ShapeDtypeStruct((heads, rows, HD), jnp.float32),
            jax.ShapeDtypeStruct((heads, rows // HD, HD), jnp.float32),
            jax.ShapeDtypeStruct((frames, 1, POSITIONS, HD), jnp.bfloat16),
        ],
        scratch_shapes=[
            pltpu.VMEM(first.shape, first.dtype),
            pltpu.VMEM(first_up.shape, first_up.dtype),
            pltpu.VMEM((1, rows, HD), jnp.float32),
            pltpu.VMEM((1, rows // HD, HD), jnp.float32),
            pltpu.SemaphoreType.DMA((2, 2)),
        ],
        compiler_params=pltpu.CompilerParams(vmem_limit_bytes=14 * 2**20),
        cost_estimate=cost(160, rows, heads, rows * heads * HD * 14),
        name="near",
    )(flags, third, second, first, first_up, far)


def merge(flags, near, logs, far, *others):
    heads, rows, _ = near.shape
    slabs = heads + sum(other.shape[1] for other in others)
    return pl.pallas_call(
        merge_kernel,
        in_specs=[SMEM] + [VMEM] * (3 + len(others)),
        out_specs=VMEM,
        out_shape=jax.ShapeDtypeStruct((rows // POSITIONS, slabs, POSITIONS, HD), jnp.bfloat16),
        compiler_params=PARAMS,
        cost_estimate=cost(0, rows, heads, rows * heads * HD * 8),
        name="merge",
    )(flags, near, logs, far, *others)


def cut_first_kernel(k_ref, v_ref, first_ref, last_ref, held_ref, first_piece, last_piece, *sems):
    in_sems, first_sems, last_sems = sems

    def fetch(which, window):
        rows = pl.ds(window * POSITIONS, POSITIONS)
        ref = (k_ref, v_ref)[which]
        return pltpu.make_async_copy(
            ref.at[rows], held_ref.at[which, rows], in_sems.at[which, window]
        )

    def stores(window):
        peers = pl.ds(window * SPAN, SPAN)
        return (
            pltpu.make_async_copy(first_piece.at[peers], first_ref.at[peers], first_sems.at[window]),
            pltpu.make_async_copy(last_piece.at[peers], last_ref.at[peers], last_sems.at[window]),
        )

    for window in range(NWIN):
        for which in range(2):
            fetch(which, window).start()
    for window in range(NWIN):
        rows = pl.ds(window * POSITIONS, POSITIONS)
        for which in range(2):
            fetch(which, window).wait()
            for part in range(SPAN):
                for head in range(PARTS):
                    lanes = pl.ds((part * PARTS + head) * HD, HD)
                    value = held_ref[which, rows, lanes]
                    if head < 2:
                        first_piece[window * SPAN + part, 2 * head + which] = value
                    else:
                        last_piece[window * SPAN + part, which] = value
        for copy in stores(window):
            copy.start()
    for window in range(NWIN):
        for copy in stores(window):
            copy.wait()


def cut_first(key, value):
    first = (NWIN * SPAN, 4, POSITIONS, HD)
    last = (NWIN * SPAN, 2, POSITIONS, HD)
    return pl.pallas_call(
        cut_first_kernel,
        in_specs=[HBM] * 2,
        out_specs=[HBM] * 2,
        out_shape=[jax.ShapeDtypeStruct(shape, jnp.bfloat16) for shape in (first, last)],
        scratch_shapes=[
            pltpu.VMEM((2,) + key.shape, jnp.bfloat16),
            pltpu.VMEM(first, jnp.bfloat16),
            pltpu.VMEM(last, jnp.bfloat16),
            pltpu.SemaphoreType.DMA((2, NWIN)),
            pltpu.SemaphoreType.DMA((NWIN,)),
            pltpu.SemaphoreType.DMA((NWIN,)),
        ],
        compiler_params=pltpu.CompilerParams(vmem_limit_bytes=60 * 2**20),
        name="cut_first",
    )(key, value)


def gate_kernel(*refs):
    del refs


def gate(space, passed, *waited):
    return pl.pallas_call(
        gate_kernel,
        in_specs=[space] + [ANY] * len(waited),
        out_specs=space,
        out_shape=jax.ShapeDtypeStruct(passed.shape, passed.dtype),
        input_output_aliases={0: 0},
        compiler_params=SMALL,
        name="gate",
    )(passed, *waited)


def cut_kernel(whole_ref, piece_ref, out_ref):
    heads = out_ref.shape[1] - piece_ref.shape[1]
    for window in range(NWIN):
        rows = pl.ds(window * POSITIONS, POSITIONS)
        for part in range(SPAN):
            for head in range(heads):
                lanes = pl.ds((part * PARTS + head) * HD, HD)
                out_ref[window * SPAN + part, head] = whole_ref[rows, lanes]
    out_ref[:, heads:] = piece_ref[...]


def cut(whole, piece, flops):
    slabs = PARTS + piece.shape[1]
    return pl.pallas_call(
        cut_kernel,
        in_specs=[VMEM] * 2,
        out_specs=VMEM,
        out_shape=jax.ShapeDtypeStruct((NWIN * SPAN, slabs, POSITIONS, HD), jnp.bfloat16),
        compiler_params=PARAMS,
        cost_estimate=pl.CostEstimate(flops=flops, bytes_accessed=2**21, transcendentals=0),
        name="cut",
    )(whole, piece)


def cut_out_kernel(whole_ref, piece_ref, out_ref, held_ref, sem):
    cut_kernel(whole_ref, piece_ref, held_ref)
    copy = pltpu.make_async_copy(held_ref, out_ref, sem)
    copy.start()
    copy.wait()


def cut_out(whole, piece):
    shape = (NWIN * SPAN, PARTS + piece.shape[1], POSITIONS, HD)
    return pl.pallas_call(
        cut_out_kernel,
        in_specs=[VMEM] * 2,
        out_specs=HBM,
        out_shape=jax.ShapeDtypeStruct(shape, jnp.bfloat16),
        scratch_shapes=[pltpu.VMEM(shape, jnp.bfloat16), pltpu.SemaphoreType.DMA],
        compiler_params=PARAMS,
        cost_estimate=pl.CostEstimate(flops=10**6, bytes_accessed=2**21, transcendentals=0),
        name="cut_out",
    )(whole, piece)


def paste_kernel(in_ref, out_ref, held_ref, sems):
    copies = []
    for window in range(NWIN):
        rows = pl.ds(window * POSITIONS, POSITIONS)
        for part in range(SPAN):
            for head in range(PARTS):
                lanes = pl.ds((part * PARTS + head) * HD, HD)
                held_ref[rows, lanes] = in_ref[window * SPAN + part, head]
        copies.append(
            pltpu.make_async_copy(held_ref.at[rows], out_ref.at[rows], sems.at[window])
        )
        copies[-1].start()
    for copy in copies:
        copy.wait()


def paste(pieces):
    return pl.pallas_call(
        paste_kernel,
        in_specs=[VMEM],
        out_specs=ANY,
        out_shape=jax.ShapeDtypeStruct((POS, HEADS * HD), jnp.bfloat16),
        scratch_shapes=[
            pltpu.VMEM((POS, HEADS * HD), jnp.bfloat16),
            pltpu.SemaphoreType.DMA((NWIN,)),
        ],
        compiler_params=PARAMS,
        name="paste",
    )(pieces)


def body(query_vectors, key_vectors, value_vectors, chosen_groups, chosen_count):
    group_devices = lax.axis_size("grp")

    def to_peers(block):
        return lax.all_to_all(block, "ctx", split_axis=0, concat_axis=0, tiled=True)

    def up(block):
        return lax.ppermute(block, "grp", [(at, at + 1) for at in range(group_devices - 1)])

    def down(block):
        return lax.ppermute(block, "grp", [(at + 1, at) for at in range(group_devices - 1)])

    later_query = down(query_vectors)
    first, last = cut_first(key_vectors, value_vectors)
    last_up = up(last)
    first = to_peers(first)
    first_up = up(first)
    flags = make_flags(chosen_groups, chosen_count)
    second = to_peers(gate(ANY, cut(later_query, last_up, 10**11), first, flags))
    third = to_peers(gate(HBM, cut_out(query_vectors, last), second))
    ahead_b = attend_ahead(flags, 1, 1, second, 2, second, 3)
    far_b = up(ahead_b)
    far_a = up(attend_ahead(flags, 2, 4, second, 0, first_up, 0, ahead_b))
    near, logs, merged = attend_near(flags, third, second, first, first_up, far_b)
    return paste(to_peers(merge(flags, near, logs, far_a, merged)))


def solution(mesh):
    in_specs = (P(("grp", "ctx"), None), P(("grp", "ctx"), None), P(("grp", "ctx"), None), P(), P())
    out_specs = P(("grp", "ctx"), None)
    return jax.shard_map(body, mesh=mesh, in_specs=in_specs, out_specs=out_specs, check_vma=False)
```
